32 devices in a mesh: leaf: 8 (over z, x), rhs: 4 (over y, core).
Axes of the slice: x: 2, y: 2, z: 4, core: 2. Of those that a mesh axis runs over, the one named last changes fastest.
Arguments:
- rhs_vectors: bfloat16 [32, 16384], P('rhs', 'leaf'), may hold values from -6 to 6
- diag_inverse: bfloat16 [16384, 2048], P('leaf'), may hold values from -1 to 2
- left_factors: bfloat16 [16384, 192], P('leaf'), may hold values from -0.375 to 0.375
- right_factors: bfloat16 [16384, 192], P('leaf'), may hold values from -0.125 to 0.125
- ranks: int32 [3], replicated, may hold values from 32 to 64, as said below
Outputs:
- solution: float32 [32, 16384], P('rhs', 'leaf')
The draws below stay inside these ranges and needn't reach their ends.
Inputs may be any that keep to these rules, and one draw needn't show every extreme that they name: `ranks`: some level has rank exactly 64.
All inputs are finite; a program needn't handle non-finite values.
Results may differ from the reference program's by a relative error of at most 0.0031.
Values sent between devices are 32-bit elements; how exact they have to be, the bound alone decides.
A program may use at most 64 MiB of HBM per device.

```python
import math
import jax
import jax.numpy as jnp
from jax import lax

M = 2048
RMAX = 64
LEVELS = 3
UNKNOWNS = 16384
NRHS = 32
N_LEAF = 8


def draw_diag_inverse(key, part):
    noise = jnp.clip(jax.random.normal(key, (UNKNOWNS, M), jnp.float32), -4.0, 4.0)
    row_id = lax.broadcasted_iota(jnp.int32, (UNKNOWNS, M), 0) % M
    col_id = lax.broadcasted_iota(jnp.int32, (UNKNOWNS, M), 1)
    eye_block = jnp.where(row_id == col_id, 1.0, 0.0).astype(jnp.float32)
    return (eye_block + noise * (0.5 / math.sqrt(M))).astype(jnp.bfloat16)


def draw_ranks(key, part):
    picks = jax.random.randint(jax.random.fold_in(key, 11), (LEVELS,), RMAX // 2, RMAX + 1)
    chosen = jax.random.randint(jax.random.fold_in(key, 12), (), 0, LEVELS)
    slots = lax.broadcasted_iota(jnp.int32, (LEVELS,), 0)
    return jnp.where(slots == chosen, RMAX, picks).astype(jnp.int32)


def shard_levels(key, extent, split, least, largest):
    factor_of = 1.0
    for dim, blocks in split:
        draws = jax.random.uniform(jax.random.fold_in(jax.random.fold_in(key, 6), dim), (blocks,), jnp.float32, least / len(split), largest / len(split))
        factor_of = factor_of * jnp.repeat(jnp.exp(draws), extent[dim] // blocks).reshape((-1,) + (1,) * (len(extent) - 1 - dim))
    return factor_of


def centred(key, shape, width, most, pieces=(), held_as=jnp.bfloat16):
    factor_of = shard_levels(key, shape, pieces, -0.22, 0.18) if pieces else 1.0
    result = jax.random.normal(key, shape, jnp.float32) * width * factor_of
    return jnp.minimum(jnp.maximum(result, -most), most).astype(held_as)


def setup_inputs(seed: int = 0) -> dict:
    arg_keys = jax.random.split(jax.random.key(seed), 6)
    return {
        "rhs_vectors": centred(arg_keys[0], (NRHS, UNKNOWNS), 1.0, 6.0, ((0, 4), (1, 8))),
        "diag_inverse": draw_diag_inverse(jax.random.fold_in(arg_keys[5], 71), 0),
        "left_factors": centred(arg_keys[2], (UNKNOWNS, LEVELS * RMAX), (RMAX * N_LEAF // 2) ** -0.5, 0.375, ((0, 8),)),
        "right_factors": centred(arg_keys[3], (UNKNOWNS, LEVELS * RMAX), M ** -0.5, 0.125, ((0, 8),)),
        "ranks": draw_ranks(jax.random.fold_in(arg_keys[5], 71), 0),
    }


best_precision = lax.Precision.HIGHEST


def reference(rhs_vectors, diag_inverse, left_factors, right_factors, ranks):
    state_rows = LEVELS * RMAX
    column_level = jnp.arange(state_rows) // RMAX
    column_rank = jnp.arange(state_rows) % RMAX
    level_table = jnp.arange(LEVELS)
    rank_of = jnp.sum(jnp.where(column_level[:, None] == level_table[None, :], ranks[None, :], 0), axis=1)
    column_keep = (column_rank < rank_of).astype(jnp.bfloat16)
    rhs_count = rhs_vectors.shape[0]
    solved = []
    projections = []
    for leaf_pos in range(N_LEAF):
        lower_row = leaf_pos * M
        inverse = diag_inverse[lower_row:lower_row + M]
        left_kept = left_factors[lower_row:lower_row + M] * column_keep[None, :]
        right_kept = (right_factors[lower_row:lower_row + M] * column_keep[None, :]).astype(jnp.float32)
        mapped = jnp.dot(inverse, left_kept, preferred_element_type=jnp.float32).astype(jnp.bfloat16)
        source = rhs_vectors[:, lower_row:lower_row + M].T
        base = jnp.dot(inverse, source, preferred_element_type=jnp.float32)
        incoming = jnp.zeros((state_rows, rhs_count), jnp.float32)
        for tree_level in range(LEVELS):
            if (leaf_pos >> tree_level) & 1:
                first_leaf = (leaf_pos >> (tree_level + 1)) << (tree_level + 1)
                gathered = projections[first_leaf]
                for sibling in range(first_leaf + 1, first_leaf + (1 << tree_level)):
                    gathered = gathered + projections[sibling]
                low_edge = tree_level * RMAX
                incoming = incoming.at[low_edge:low_edge + RMAX].set(gathered[low_edge:low_edge + RMAX])
        answer = base - jnp.dot(mapped.astype(jnp.float32), incoming, precision=best_precision)
        projections.append(jnp.dot(right_kept.T, answer, precision=best_precision))
        solved.append(answer.T)
    return jnp.concatenate(solved, axis=1)
```

```python
import functools

import jax
import jax.numpy as jnp
from jax import lax
from jax.experimental import pallas as pl
from jax.experimental.pallas import tpu as pltpu
from jax.sharding import PartitionSpec as P

LANES = 128
F32 = jnp.float32
BF16 = jnp.bfloat16


def split(x):
    high = x.astype(BF16)
    return high, (x - high.astype(F32)).astype(BF16)


def dot(a, b):
    return jnp.dot(a, b, preferred_element_type=F32)


def dot_split(a, b):
    a_high, a_low = split(a)
    b_high, b_low = split(b)
    return dot(a_high, b_high) + (dot(a_high, b_low) + dot(a_low, b_high))


def kernel(
    levels, rank_top, chunk,
    ranks_ref, b_ref, d_hbm, u_hbm, v_hbm, y_ref,
    d_buf, u_buf, v_buf, x_ref, acc_ref, wt_ref, c_ref, r_ref, total, got,
    d_sem, u_sem, v_sem, send_sem, got_sem,
):
    me = lax.axis_index("leaf")
    rows = d_buf.shape[0]
    chunks = rows // chunk
    state = u_buf.shape[1]
    count = b_ref.shape[0]
    tiles = total.shape[0]
    bits = [lax.rem(lax.div(me, 1 << l), 2) for l in range(levels)]

    def d_copy(m):
        at = pl.ds(pl.multiple_of(m * chunk, chunk), chunk)
        return pltpu.make_async_copy(d_hbm.at[at, :], d_buf.at[at, :], d_sem.at[m])

    u_copy = pltpu.make_async_copy(u_hbm, u_buf, u_sem)
    v_copy = pltpu.make_async_copy(v_hbm, v_buf, v_sem)
    u_copy.start()
    d_copy(0).start()
    v_copy.start()
    for m in range(1, chunks):
        d_copy(m).start()

    def sender_of(l):
        span = 2 << l
        return lax.div(me, span) * span + ((1 << l) - 1)

    def is_last(l):
        return lax.rem(me, 1 << l) == (1 << l) - 1

    got[...] = jnp.zeros_like(got)
    total[...] = jnp.zeros_like(total)
    barrier = pltpu.get_barrier_semaphore()
    for l in range(levels):
        @pl.when(bits[l] == 1)
        def _():
            pl.semaphore_signal(
                barrier, inc=1, device_id={"leaf": sender_of(l)},
                device_id_type=pl.DeviceIdType.MESH,
            )

    edge = state // LANES * LANES
    above = state - edge
    b = b_ref[...].astype(F32)
    pieces = [b, jnp.zeros((LANES - above - count, rows), F32)]
    if above:
        pieces = [jnp.zeros((above, rows), F32)] + pieces
    x_ref[:, edge:edge + LANES] = jnp.concatenate(pieces, axis=0).T.astype(BF16)
    u_copy.wait()
    if edge:
        x_ref[:, 0:edge] = u_buf[:, 0:edge]
    if above:
        x_ref[:, edge:state] = u_buf[:, edge:state]
    r_ref[...] = jnp.zeros_like(r_ref)

    def multiply(m):
        at = pl.ds(pl.multiple_of(m * chunk, chunk), chunk)
        return dot(d_buf[at, :], x_ref[...])

    def project(m, block):
        at = pl.ds(pl.multiple_of(m * chunk, chunk), chunk)
        turned = block.T
        w = turned[0:state].astype(BF16)
        c = turned[state:state + count]
        c_ref[:, at] = c
        high = c.astype(BF16).astype(F32)
        both = jnp.concatenate([high, c - high], axis=0).astype(BF16)
        wt_ref[:, at] = w
        v = v_buf[at, :]
        r_ref[0:state, :] += dot(w, v)
        r_ref[state:state + 2 * count, :] += dot(both, v)

    d_copy(0).wait()
    acc_ref[0] = multiply(0)
    v_copy.wait()

    def body(m, carry):
        d_copy(m).wait()
        before = acc_ref[lax.rem(m + 1, 2)]
        block = multiply(m)
        project(m - 1, before)
        acc_ref[lax.rem(m, 2)] = block
        return carry

    lax.fori_loop(1, chunks, body, 0)
    project(chunks - 1, acc_ref[(chunks - 1) % 2])

    lane = lax.broadcasted_iota(jnp.int32, (1, state), 1)
    limit = jnp.zeros((1, state), jnp.int32)
    for l in range(levels):
        limit = jnp.where(lane // rank_top == l, ranks_ref[l], limit)
    r = jnp.where(lane % rank_top < limit, r_ref[...], 0.0)
    for t in range(tiles):
        wide = min(LANES, state - t * LANES)
        part = r[:, t * LANES:t * LANES + wide]
        total[t, 0:count, 0:wide] = (
            part[state:state + count] + part[state + count:state + 2 * count]
        )
        total[t, count:count + state, 0:wide] = -part[0:state]

    def tile_of(l):
        return l * rank_top // LANES

    def tile_used(l, t):
        used = bits[0] < 0
        for c in range(l + 1, levels):
            if tile_of(c) == t:
                used = jnp.logical_or(used, bits[c] == 0)
        return used

    def row_block(m):
        if m is None:
            return pl.ds(0, count)
        return pl.ds(count + m * rank_top, rank_top)

    def copies(l):
        out = []
        last = (1 << l) - 1
        first = lax.div(me, 2 << l) * (2 << l) + (1 << l)
        for place in range(last, -1, -1):
            for m in [None] + list(range(l + 1, levels)):
                for t in range(tiles):
                    if t != tile_of(l) and (place != last or all(tile_of(c) != t for c in range(l + 1, levels))):
                        continue
                    condition = []
                    if m is not None:
                        condition.append(bits[m] == 1)
                    if t != tile_of(l):
                        condition.append(tile_used(l, t))
                    slot = 0 if m is None else m + 1
                    out.append((place, condition, pltpu.make_async_remote_copy(
                        src_ref=total.at[t, row_block(m), :],
                        dst_ref=got.at[l, t, row_block(m), :],
                        send_sem=send_sem.at[len(out)],
                        recv_sem=got_sem.at[l, t, slot],
                        device_id={"leaf": first + place},
                        device_id_type=pl.DeviceIdType.MESH,
                    )))
        return out

    def guarded(conditions, action):
        if conditions:
            pl.when(functools.reduce(jnp.logical_and, conditions))(action)
        else:
            action()

    def receive(l):
        for place, condition, copy in copies(l):
            if place != (1 << l) - 1:
                continue
            guarded(condition, copy.wait_recv)

    def receive_narrow(l):
        t = tile_of(l)
        for m in [None] + list(range(l + 1, levels)):
            copy = pltpu.make_async_remote_copy(
                src_ref=total.at[t, row_block(m), :],
                dst_ref=got.at[l, t, row_block(m), :],
                send_sem=send_sem.at[0],
                recv_sem=got_sem.at[l, t, 0 if m is None else m + 1],
                device_id={"leaf": sender_of(l)},
                device_id_type=pl.DeviceIdType.MESH,
            )
            guarded([] if m is None else [bits[m] == 1], copy.wait_recv)

    def join(l):
        own = tile_of(l)
        start = l * rank_top - own * LANES
        row = lax.broadcasted_iota(jnp.int32, (LANES, LANES), 0)
        inside = jnp.logical_and(row >= start, row < start + rank_top)

        def update(lo, hi):
            factor = got[l, own, lo:hi, :]
            for t in range(tiles):
                if all(tile_of(c) != t for c in range(l + 1, levels)):
                    continue
                at = count + own * LANES
                step = jnp.where(inside, total[t, at:at + LANES, :], 0.0)
                total[t, lo:hi, :] = (
                    total[t, lo:hi, :] + got[l, t, lo:hi, :] + dot_split(factor, step)
                )

        update(0, count)
        if l + 1 < levels:
            @pl.when(lax.div(me, 2 << l) > 0)
            def _():
                update(count + (l + 1) * rank_top, count + state)

    for l in range(levels):
        sends = jnp.logical_and(is_last(l), bits[l] == 0)
        if l:
            takes = jnp.logical_and(is_last(l), bits[l] == 1)
            others = jnp.logical_and(jnp.logical_not(is_last(l)), bits[l] == 1)
        else:
            takes, others = bits[l] == 1, None

        @pl.when(sends)
        def _():
            pl.semaphore_wait(barrier, 1 << l)
            for _, condition, copy in copies(l):
                guarded(condition, copy.start)

        @pl.when(takes)
        def _():
            receive(l)
            if l + 1 < levels:
                join(l)

        if others is not None:
            @pl.when(others)
            def _():
                receive_narrow(l)

    wide = tiles * LANES
    lane = lax.broadcasted_iota(jnp.int32, (1, LANES), 1)
    parts = [jnp.zeros((count, LANES), F32)] * tiles
    for l in range(levels - 1, -1, -1):
        t = tile_of(l)
        value = got[l, t, 0:count, :]
        if l + 1 < levels:
            value = value + dot_split(
                jnp.concatenate(parts, axis=1), got[l, t, count:count + wide, :]
            )
        start = l * rank_top - t * LANES
        inside = jnp.logical_and(lane >= start, lane < start + rank_top)
        parts[t] = jnp.where(inside, value, parts[t])
    p = jnp.concatenate(parts, axis=1)[:, 0:state]
    high = p.astype(BF16).astype(F32)
    both = jnp.concatenate([high, p - high], axis=0).astype(BF16)
    moved = dot(both, wt_ref[...])
    y_ref[...] = c_ref[...] - (moved[0:count] + moved[count:2 * count])

    for l in range(levels):
        @pl.when(jnp.logical_and(is_last(l), bits[l] == 0))
        def _():
            for _, condition, copy in copies(l):
                guarded(condition, copy.wait_send)


def on_device(rhs_vectors, diag_inverse, left_factors, right_factors, ranks):
    leaves = lax.axis_size("leaf")
    levels = leaves.bit_length() - 1
    count, rows = rhs_vectors.shape
    state = left_factors.shape[1]
    rank_top = state // levels
    tiles = pl.cdiv(state, LANES)
    wide = pl.cdiv(state + count, LANES) * LANES
    chunk = rows // 8
    most = 0
    for l in range(levels):
        most = max(most, ((1 << l) - 1 + tiles) * (levels - l))
    vmem = pl.BlockSpec(memory_space=pltpu.VMEM)
    hbm = pl.BlockSpec(memory_space=pl.ANY)
    return pl.pallas_call(
        functools.partial(kernel, levels, rank_top, chunk),
        out_shape=jax.ShapeDtypeStruct((count, rows), F32),
        in_specs=[pl.BlockSpec(memory_space=pltpu.SMEM), vmem, hbm, hbm, hbm],
        out_specs=vmem,
        scratch_shapes=[
            pltpu.VMEM(diag_inverse.shape, BF16),
            pltpu.VMEM((rows, state), BF16),
            pltpu.VMEM((rows, state), BF16),
            pltpu.VMEM((rows, wide), BF16),
            pltpu.VMEM((2, chunk, wide), F32),
            pltpu.VMEM((state, rows), BF16),
            pltpu.VMEM((count, rows), F32),
            pltpu.VMEM((state + 2 * count, state), F32),
            pltpu.VMEM((tiles, count + tiles * LANES, LANES), F32),
            pltpu.VMEM((levels, tiles, count + tiles * LANES, LANES), F32),
            pltpu.SemaphoreType.DMA((rows // chunk,)),
            pltpu.SemaphoreType.DMA,
            pltpu.SemaphoreType.DMA,
            pltpu.SemaphoreType.DMA((most,)),
            pltpu.SemaphoreType.DMA((levels, tiles, levels + 1)),
        ],
        compiler_params=pltpu.CompilerParams(
            collective_id=0, has_side_effects=True, vmem_limit_bytes=56 * 1024 * 1024
        ),
        cost_estimate=pl.CostEstimate(
            flops=2 * rows * rows * wide, bytes_accessed=2 * rows * (rows + 2 * state), transcendentals=0
        ),
    )(ranks, rhs_vectors, diag_inverse, left_factors, right_factors)


def solution(mesh):
    in_specs = (P("rhs", "leaf"), P("leaf", None), P("leaf", None), P("leaf", None), P())
    return jax.shard_map(
        on_device, mesh=mesh, in_specs=in_specs, out_specs=P("rhs", "leaf"), check_vma=False
    )
```

```python
import functools

import jax
import jax.numpy as jnp
from jax import lax
from jax.experimental import pallas as pl
from jax.experimental.pallas import tpu as pltpu
from jax.sharding import PartitionSpec as P

LANES = 128
F32 = jnp.float32
BF16 = jnp.bfloat16


def split(x):
    high = x.astype(BF16)
    return high, (x - high.astype(F32)).astype(BF16)


def dot(a, b):
    return jnp.dot(a, b, preferred_element_type=F32)


def dot_turned(a, b):
    return lax.dot_general(a, b, (((1,), (1,)), ((), ())), preferred_element_type=F32)


def dot_split(a, b):
    a_high, a_low = split(a)
    b_high, b_low = split(b)
    return dot(a_high, b_high) + (dot(a_high, b_low) + dot(a_low, b_high))


def kernel(
    levels, rank_top, chunk,
    ranks_ref, b_ref, d_hbm, u_hbm, v_hbm, c_ref, moved_ref,
    d_buf, v_buf, x_ref, acc_ref, wt_ref, r_ref, total, got,
    d_sem, u_sem, v_sem, send_sem, got_sem,
):
    me = lax.axis_index("leaf")
    rows = d_buf.shape[0]
    chunks = rows // chunk
    state = v_buf.shape[0]
    count = b_ref.shape[0]
    tiles = total.shape[0]
    bits = [lax.rem(lax.div(me, 1 << l), 2) for l in range(levels)]

    def d_copy(m):
        at = pl.ds(pl.multiple_of(m * chunk, chunk), chunk)
        return pltpu.make_async_copy(d_hbm.at[at, :], d_buf.at[at, :], d_sem.at[m])

    u_copy = pltpu.make_async_copy(u_hbm, x_ref.at[pl.ds(0, state), :], u_sem)
    v_copy = pltpu.make_async_copy(v_hbm, v_buf, v_sem)
    u_copy.start()
    d_copy(0).start()
    v_copy.start()
    for m in range(1, chunks):
        d_copy(m).start()

    def sender_of(l):
        span = 2 << l
        return lax.div(me, span) * span + ((1 << l) - 1)

    def is_last(l):
        return lax.rem(me, 1 << l) == (1 << l) - 1

    got[...] = jnp.zeros_like(got)
    total[...] = jnp.zeros_like(total)
    barrier = pltpu.get_barrier_semaphore()
    for l in range(levels):
        @pl.when(bits[l] == 1)
        def _():
            pl.semaphore_signal(
                barrier, inc=1, device_id={"leaf": sender_of(l)},
                device_id_type=pl.DeviceIdType.MESH,
            )

    b = b_ref[...].astype(F32)
    x_ref[state:state + 2 * count, :] = jnp.concatenate([b, b], axis=0).astype(BF16)
    u_copy.wait()
    r_ref[...] = jnp.zeros_like(r_ref)

    def multiply(m):
        at = pl.ds(pl.multiple_of(m * chunk, chunk), chunk)
        return dot_turned(x_ref[...], d_buf[at, :])

    def project(m, block):
        at = pl.ds(pl.multiple_of(m * chunk, chunk), chunk)
        w = block[0:state].astype(BF16)
        twice = block[state:state + 2 * count]
        c_ref[:, at] = twice[0:count]
        high = twice.astype(BF16).astype(F32)
        row = lax.broadcasted_iota(jnp.int32, twice.shape, 0)
        both = jnp.where(row < count, high, twice - high).astype(BF16)
        wt_ref[:, at] = w
        r_ref[...] += dot_turned(jnp.concatenate([w, both], axis=0), v_buf[:, at])

    d_copy(0).wait()
    acc_ref[0] = multiply(0)
    v_copy.wait()

    def body(m, carry):
        d_copy(m).wait()
        before = acc_ref[lax.rem(m + 1, 2)]
        block = multiply(m)
        project(m - 1, before)
        acc_ref[lax.rem(m, 2)] = block
        return carry

    lax.fori_loop(1, chunks, body, 0)
    project(chunks - 1, acc_ref[(chunks - 1) % 2])

    lane = lax.broadcasted_iota(jnp.int32, (1, state), 1)
    limit = jnp.zeros((1, state), jnp.int32)
    for l in range(levels):
        limit = jnp.where(lane // rank_top == l, ranks_ref[l], limit)
    r = jnp.where(lane % rank_top < limit, r_ref[...], 0.0)
    for t in range(tiles):
        wide = min(LANES, state - t * LANES)
        part = r[:, t * LANES:t * LANES + wide]
        total[t, 0:count, 0:wide] = (
            part[state:state + count] + part[state + count:state + 2 * count]
        )
        total[t, count:count + state, 0:wide] = -part[0:state]

    def tile_of(l):
        return l * rank_top // LANES

    def tile_used(l, t):
        used = bits[0] < 0
        for c in range(l + 1, levels):
            if tile_of(c) == t:
                used = jnp.logical_or(used, bits[c] == 0)
        return used

    def row_block(m):
        if m is None:
            return pl.ds(0, count)
        return pl.ds(count + m * rank_top, rank_top)

    def copies(l):
        out = []
        last = (1 << l) - 1
        first = lax.div(me, 2 << l) * (2 << l) + (1 << l)
        for place in range(last, -1, -1):
            for m in [None] + list(range(l + 1, levels)):
                for t in range(tiles):
                    if t != tile_of(l) and (place != last or all(tile_of(c) != t for c in range(l + 1, levels))):
                        continue
                    condition = []
                    if m is not None:
                        condition.append(bits[m] == 1)
                    if t != tile_of(l):
                        condition.append(tile_used(l, t))
                    slot = 0 if m is None else m + 1
                    out.append((place, condition, pltpu.make_async_remote_copy(
                        src_ref=total.at[t, row_block(m), :],
                        dst_ref=got.at[l, t, row_block(m), :],
                        send_sem=send_sem.at[len(out)],
                        recv_sem=got_sem.at[l, t, slot],
                        device_id={"leaf": first + place},
                        device_id_type=pl.DeviceIdType.MESH,
                    )))
        return out

    def guarded(conditions, action):
        if conditions:
            pl.when(functools.reduce(jnp.logical_and, conditions))(action)
        else:
            action()

    def receive(l):
        for place, condition, copy in copies(l):
            if place != (1 << l) - 1:
                continue
            guarded(condition, copy.wait_recv)

    def receive_narrow(l):
        t = tile_of(l)
        for m in [None] + list(range(l + 1, levels)):
            copy = pltpu.make_async_remote_copy(
                src_ref=total.at[t, row_block(m), :],
                dst_ref=got.at[l, t, row_block(m), :],
                send_sem=send_sem.at[0],
                recv_sem=got_sem.at[l, t, 0 if m is None else m + 1],
                device_id={"leaf": sender_of(l)},
                device_id_type=pl.DeviceIdType.MESH,
            )
            guarded([] if m is None else [bits[m] == 1], copy.wait_recv)

    def join(l):
        own = tile_of(l)
        start = l * rank_top - own * LANES
        row = lax.broadcasted_iota(jnp.int32, (LANES, LANES), 0)
        inside = jnp.logical_and(row >= start, row < start + rank_top)

        def update(lo, hi):
            factor = got[l, own, lo:hi, :]
            for t in range(tiles):
                if all(tile_of(c) != t for c in range(l + 1, levels)):
                    continue
                at = count + own * LANES
                step = jnp.where(inside, total[t, at:at + LANES, :], 0.0)
                total[t, lo:hi, :] = (
                    total[t, lo:hi, :] + got[l, t, lo:hi, :] + dot_split(factor, step)
                )

        update(0, count)
        if l + 1 < levels:
            @pl.when(lax.div(me, 2 << l) > 0)
            def _():
                update(count + (l + 1) * rank_top, count + state)

    for l in range(levels):
        sends = jnp.logical_and(is_last(l), bits[l] == 0)
        if l:
            takes = jnp.logical_and(is_last(l), bits[l] == 1)
            others = jnp.logical_and(jnp.logical_not(is_last(l)), bits[l] == 1)
        else:
            takes, others = bits[l] == 1, None

        @pl.when(sends)
        def _():
            pl.semaphore_wait(barrier, 1 << l)
            for _, condition, copy in copies(l):
                guarded(condition, copy.start)

        @pl.when(takes)
        def _():
            receive(l)
            if l + 1 < levels:
                join(l)

        if others is not None:
            @pl.when(others)
            def _():
                receive_narrow(l)

    wide = tiles * LANES
    lane = lax.broadcasted_iota(jnp.int32, (1, LANES), 1)
    parts = [jnp.zeros((count, LANES), F32)] * tiles
    for l in range(levels - 1, -1, -1):
        t = tile_of(l)
        value = got[l, t, 0:count, :]
        if l + 1 < levels:
            value = value + dot_split(
                jnp.concatenate(parts, axis=1), got[l, t, count:count + wide, :]
            )
        start = l * rank_top - t * LANES
        inside = jnp.logical_and(lane >= start, lane < start + rank_top)
        parts[t] = jnp.where(inside, value, parts[t])
    p = jnp.concatenate(parts, axis=1)[:, 0:state]
    high = p.astype(BF16).astype(F32)
    both = jnp.concatenate([high, p - high], axis=0).astype(BF16)
    moved = dot(both, wt_ref[...])
    moved_ref[...] = moved[0:count] + moved[count:2 * count]

    for l in range(levels):
        @pl.when(jnp.logical_and(is_last(l), bits[l] == 0))
        def _():
            for _, condition, copy in copies(l):
                guarded(condition, copy.wait_send)


def on_device(rhs_vectors, diag_inverse, left_factors, right_factors, ranks):
    leaves = lax.axis_size("leaf")
    levels = leaves.bit_length() - 1
    count, rows = rhs_vectors.shape
    state = left_factors.shape[1]
    rank_top = state // levels
    tiles = pl.cdiv(state, LANES)
    chunk = rows // 8
    most = 0
    for l in range(levels):
        most = max(most, ((1 << l) - 1 + tiles) * (levels - l))
    vmem = pl.BlockSpec(memory_space=pltpu.VMEM)
    hbm = pl.BlockSpec(memory_space=pl.ANY)
    base, moved = pl.pallas_call(
        functools.partial(kernel, levels, rank_top, chunk),
        out_shape=[jax.ShapeDtypeStruct((count, rows), F32)] * 2,
        in_specs=[pl.BlockSpec(memory_space=pltpu.SMEM), vmem, hbm, hbm, hbm],
        out_specs=[vmem, vmem],
        scratch_shapes=[
            pltpu.VMEM(diag_inverse.shape, BF16),
            pltpu.VMEM((state, rows), BF16),
            pltpu.VMEM((state + 2 * count, rows), BF16),
            pltpu.VMEM((2, state + 2 * count, chunk), F32),
            pltpu.VMEM((state, rows), BF16),
            pltpu.VMEM((state + 2 * count, state), F32),
            pltpu.VMEM((tiles, count + tiles * LANES, LANES), F32),
            pltpu.VMEM((levels, tiles, count + tiles * LANES, LANES), F32),
            pltpu.SemaphoreType.DMA((rows // chunk,)),
            pltpu.SemaphoreType.DMA,
            pltpu.SemaphoreType.DMA,
            pltpu.SemaphoreType.DMA((most,)),
            pltpu.SemaphoreType.DMA((levels, tiles, levels + 1)),
        ],
        compiler_params=pltpu.CompilerParams(
            collective_id=0, has_side_effects=True, vmem_limit_bytes=56 * 1024 * 1024
        ),
        cost_estimate=pl.CostEstimate(
            flops=2 * rows * rows * (state + count), bytes_accessed=2 * rows * (rows + 2 * state), transcendentals=0
        ),
    )(ranks, rhs_vectors, diag_inverse, left_factors.T, right_factors.T)
    return base - moved


def solution(mesh):
    in_specs = (P("rhs", "leaf"), P("leaf", None), P("leaf", None), P("leaf", None), P())
    return jax.shard_map(
        on_device, mesh=mesh, in_specs=in_specs, out_specs=P("rhs", "leaf"), check_vma=False
    )
```

```python
import functools

import jax
import jax.numpy as jnp
from jax import lax
from jax.experimental import pallas as pl
from jax.experimental.pallas import tpu as pltpu
from jax.sharding import PartitionSpec as P

LANES = 128
F32 = jnp.float32
BF16 = jnp.bfloat16


def split(x):
    high = x.astype(BF16)
    return high, (x - high.astype(F32)).astype(BF16)


def dot(a, b):
    return jnp.dot(a, b, preferred_element_type=F32)


def dot_turned(a, b):
    return lax.dot_general(a, b, (((1,), (1,)), ((), ())), preferred_element_type=F32)


def dot_split(a, b):
    a_high, a_low = split(a)
    b_high, b_low = split(b)
    return dot(a_high, b_high) + (dot(a_high, b_low) + dot(a_low, b_high))


def kernel(
    levels, rank_top, chunk,
    ranks_ref, b_ref, d_hbm, u_hbm, v_hbm, c_ref, moved_ref,
    d_buf, v_buf, x_ref, wt_ref, r_ref, total, got,
    d_sem, u_sem, v_sem, send_sem, got_sem,
):
    me = lax.axis_index("leaf")
    rows = d_buf.shape[0]
    chunks = rows // chunk
    state = v_buf.shape[0]
    count = b_ref.shape[0]
    tiles = total.shape[0]
    bits = [lax.rem(lax.div(me, 1 << l), 2) for l in range(levels)]

    def d_copy(m):
        at = pl.ds(m * chunk, chunk)
        return pltpu.make_async_copy(d_hbm.at[at, :], d_buf.at[at, :], d_sem.at[m])

    u_copy = pltpu.make_async_copy(u_hbm, x_ref.at[pl.ds(0, state), :], u_sem)
    v_copy = pltpu.make_async_copy(v_hbm, v_buf, v_sem)
    u_copy.start()
    d_copy(0).start()
    v_copy.start()
    for m in range(1, chunks):
        d_copy(m).start()

    def sender_of(l):
        span = 2 << l
        return lax.div(me, span) * span + ((1 << l) - 1)

    def is_last(l):
        return lax.rem(me, 1 << l) == (1 << l) - 1

    got[...] = jnp.zeros_like(got)
    total[...] = jnp.zeros_like(total)
    barrier = pltpu.get_barrier_semaphore()
    for l in range(levels):
        @pl.when(bits[l] == 1)
        def _():
            pl.semaphore_signal(
                barrier, inc=1, device_id={"leaf": sender_of(l)},
                device_id_type=pl.DeviceIdType.MESH,
            )

    b = b_ref[...].astype(F32)
    x_ref[state:state + 2 * count, :] = jnp.concatenate([b, b], axis=0).astype(BF16)
    u_copy.wait()
    r_ref[...] = jnp.zeros_like(r_ref)

    def multiply(m):
        at = pl.ds(m * chunk, chunk)
        return dot_turned(x_ref[...], d_buf[at, :])

    def project(m, block):
        at = pl.ds(m * chunk, chunk)
        w = block[0:state].astype(BF16)
        twice = block[state:state + 2 * count]
        c_ref[:, at] = twice[0:count]
        high = twice.astype(BF16).astype(F32)
        row = lax.broadcasted_iota(jnp.int32, twice.shape, 0)
        both = jnp.where(row < count, high, twice - high).astype(BF16)
        wt_ref[:, at] = w
        r_ref[...] += dot_turned(jnp.concatenate([w, both], axis=0), v_buf[:, at])

    block = None
    for m in range(chunks):
        d_copy(m).wait()
        if m == 1:
            v_copy.wait()
        after = multiply(m)
        if m:
            project(m - 1, block)
        block = after
    project(chunks - 1, block)

    lane = lax.broadcasted_iota(jnp.int32, (1, state), 1)
    limit = jnp.zeros((1, state), jnp.int32)
    for l in range(levels):
        limit = jnp.where(lane // rank_top == l, ranks_ref[l], limit)
    r = jnp.where(lane % rank_top < limit, r_ref[...], 0.0)
    for t in range(tiles):
        wide = min(LANES, state - t * LANES)
        part = r[:, t * LANES:t * LANES + wide]
        total[t, 0:count, 0:wide] = (
            part[state:state + count] + part[state + count:state + 2 * count]
        )
        total[t, count:count + state, 0:wide] = -part[0:state]

    def tile_of(l):
        return l * rank_top // LANES

    def tile_used(l, t):
        used = bits[0] < 0
        for c in range(l + 1, levels):
            if tile_of(c) == t:
                used = jnp.logical_or(used, bits[c] == 0)
        return used

    def row_block(m):
        if m is None:
            return pl.ds(0, count)
        return pl.ds(count + m * rank_top, rank_top)

    def copies(l):
        out = []
        last = (1 << l) - 1
        first = lax.div(me, 2 << l) * (2 << l) + (1 << l)
        for place in range(last, -1, -1):
            for m in [None] + list(range(l + 1, levels)):
                for t in range(tiles):
                    if t != tile_of(l) and (place != last or all(tile_of(c) != t for c in range(l + 1, levels))):
                        continue
                    condition = []
                    if m is not None:
                        condition.append(bits[m] == 1)
                    if t != tile_of(l):
                        condition.append(tile_used(l, t))
                    slot = 0 if m is None else m + 1
                    out.append((place, condition, pltpu.make_async_remote_copy(
                        src_ref=total.at[t, row_block(m), :],
                        dst_ref=got.at[l, t, row_block(m), :],
                        send_sem=send_sem.at[len(out)],
                        recv_sem=got_sem.at[l, t, slot],
                        device_id={"leaf": first + place},
                        device_id_type=pl.DeviceIdType.MESH,
                    )))
        return out

    def guarded(conditions, action):
        if conditions:
            pl.when(functools.reduce(jnp.logical_and, conditions))(action)
        else:
            action()

    def receive(l):
        for place, condition, copy in copies(l):
            if place != (1 << l) - 1:
                continue
            guarded(condition, copy.wait_recv)

    def receive_narrow(l):
        t = tile_of(l)
        for m in [None] + list(range(l + 1, levels)):
            copy = pltpu.make_async_remote_copy(
                src_ref=total.at[t, row_block(m), :],
                dst_ref=got.at[l, t, row_block(m), :],
                send_sem=send_sem.at[0],
                recv_sem=got_sem.at[l, t, 0 if m is None else m + 1],
                device_id={"leaf": sender_of(l)},
                device_id_type=pl.DeviceIdType.MESH,
            )
            guarded([] if m is None else [bits[m] == 1], copy.wait_recv)

    def join(l):
        own = tile_of(l)
        start = l * rank_top - own * LANES
        row = lax.broadcasted_iota(jnp.int32, (LANES, LANES), 0)
        inside = jnp.logical_and(row >= start, row < start + rank_top)

        def update(lo, hi):
            factor = got[l, own, lo:hi, :]
            for t in range(tiles):
                if all(tile_of(c) != t for c in range(l + 1, levels)):
                    continue
                at = count + own * LANES
                step = jnp.where(inside, total[t, at:at + LANES, :], 0.0)
                total[t, lo:hi, :] = (
                    total[t, lo:hi, :] + got[l, t, lo:hi, :] + dot_split(factor, step)
                )

        update(0, count)
        if l + 1 < levels:
            @pl.when(lax.div(me, 2 << l) > 0)
            def _():
                update(count + (l + 1) * rank_top, count + state)

    for l in range(levels):
        sends = jnp.logical_and(is_last(l), bits[l] == 0)
        if l:
            takes = jnp.logical_and(is_last(l), bits[l] == 1)
            others = jnp.logical_and(jnp.logical_not(is_last(l)), bits[l] == 1)
        else:
            takes, others = bits[l] == 1, None

        @pl.when(sends)
        def _():
            pl.semaphore_wait(barrier, 1 << l)
            for _, condition, copy in copies(l):
                guarded(condition, copy.start)

        @pl.when(takes)
        def _():
            receive(l)
            if l + 1 < levels:
                join(l)

        if others is not None:
            @pl.when(others)
            def _():
                receive_narrow(l)

    wide = tiles * LANES
    lane = lax.broadcasted_iota(jnp.int32, (1, LANES), 1)
    parts = [jnp.zeros((count, LANES), F32)] * tiles
    for l in range(levels - 1, -1, -1):
        t = tile_of(l)
        value = got[l, t, 0:count, :]
        if l + 1 < levels:
            value = value + dot_split(
                jnp.concatenate(parts, axis=1), got[l, t, count:count + wide, :]
            )
        start = l * rank_top - t * LANES
        inside = jnp.logical_and(lane >= start, lane < start + rank_top)
        parts[t] = jnp.where(inside, value, parts[t])
    p = jnp.concatenate(parts, axis=1)[:, 0:state]
    high = p.astype(BF16).astype(F32)
    both = jnp.concatenate([high, p - high], axis=0).astype(BF16)
    moved = dot(both, wt_ref[...])
    moved_ref[...] = moved[0:count] + moved[count:2 * count]

    for l in range(levels):
        @pl.when(jnp.logical_and(is_last(l), bits[l] == 0))
        def _():
            for _, condition, copy in copies(l):
                guarded(condition, copy.wait_send)


def on_device(rhs_vectors, diag_inverse, left_factors, right_factors, ranks):
    leaves = lax.axis_size("leaf")
    levels = leaves.bit_length() - 1
    count, rows = rhs_vectors.shape
    state = left_factors.shape[1]
    rank_top = state // levels
    tiles = pl.cdiv(state, LANES)
    chunk = rows // 4
    most = 0
    for l in range(levels):
        most = max(most, ((1 << l) - 1 + tiles) * (levels - l))
    vmem = pl.BlockSpec(memory_space=pltpu.VMEM)
    hbm = pl.BlockSpec(memory_space=pltpu.HBM)
    base, moved = pl.pallas_call(
        functools.partial(kernel, levels, rank_top, chunk),
        out_shape=[jax.ShapeDtypeStruct((count, rows), F32)] * 2,
        in_specs=[pl.BlockSpec(memory_space=pltpu.SMEM), vmem, hbm, hbm, hbm],
        out_specs=[vmem, vmem],
        scratch_shapes=[
            pltpu.VMEM(diag_inverse.shape, BF16),
            pltpu.VMEM((state, rows), BF16),
            pltpu.VMEM((state + 2 * count, rows), BF16),
            pltpu.VMEM((state, rows), BF16),
            pltpu.VMEM((state + 2 * count, state), F32),
            pltpu.VMEM((tiles, count + tiles * LANES, LANES), F32),
            pltpu.VMEM((levels, tiles, count + tiles * LANES, LANES), F32),
            pltpu.SemaphoreType.DMA((rows // chunk,)),
            pltpu.SemaphoreType.DMA,
            pltpu.SemaphoreType.DMA,
            pltpu.SemaphoreType.DMA((most,)),
            pltpu.SemaphoreType.DMA((levels, tiles, levels + 1)),
        ],
        compiler_params=pltpu.CompilerParams(
            collective_id=0, has_side_effects=True, vmem_limit_bytes=55040 * 1024
        ),
        cost_estimate=pl.CostEstimate(
            flops=2 * rows * rows * (state + count), bytes_accessed=2 * rows * (rows + 2 * state), transcendentals=0
        ),
    )(ranks, rhs_vectors, diag_inverse, left_factors.T, right_factors.T)
    return base - moved


def solution(mesh):
    in_specs = (P("rhs", "leaf"), P("leaf", None), P("leaf", None), P("leaf", None), P())
    return jax.shard_map(
        on_device, mesh=mesh, in_specs=in_specs, out_specs=P("rhs", "leaf"), check_vma=False
    )
```

```python
import functools

import jax
import jax.numpy as jnp
from jax import lax
from jax.experimental import pallas as pl
from jax.experimental.pallas import tpu as pltpu
from jax.sharding import PartitionSpec as P

LANES = 128
F32 = jnp.float32
BF16 = jnp.bfloat16


def split(x):
    high = x.astype(BF16)
    return high, (x - high.astype(F32)).astype(BF16)


def dot(a, b):
    return jnp.dot(a, b, preferred_element_type=F32)


def dot_split(a, b):
    a_high, a_low = split(a)
    b_high, b_low = split(b)
    return dot(a_high, b_high) + (dot(a_high, b_low) + dot(a_low, b_high))


def kernel(
    levels, rank_top, chunk,
    ranks_ref, b_ref, d_hbm, u_hbm, v_hbm, c_ref, moved_ref,
    d_buf, v_buf, turned_ref, x_ref, w_ref, tall_ref, wt_ref, total, got,
    d_sem, u_sem, v_sem, send_sem, got_sem,
):
    me = lax.axis_index("leaf")
    rows = d_buf.shape[0]
    chunks = rows // chunk
    state = v_buf.shape[0]
    count = b_ref.shape[0]
    tiles = total.shape[0]
    bits = [lax.rem(lax.div(me, 1 << l), 2) for l in range(levels)]

    def d_copy(m):
        at = pl.ds(m * chunk, chunk)
        return pltpu.make_async_copy(d_hbm.at[at, :], d_buf.at[at, :], d_sem.at[m])

    u_copy = pltpu.make_async_copy(u_hbm, turned_ref.at[pl.ds(0, state), :], u_sem)
    v_copy = pltpu.make_async_copy(v_hbm, v_buf, v_sem)
    u_copy.start()
    d_copy(0).start()
    v_copy.start()
    for m in range(1, chunks):
        d_copy(m).start()

    def sender_of(l):
        span = 2 << l
        return lax.div(me, span) * span + ((1 << l) - 1)

    def is_last(l):
        return lax.rem(me, 1 << l) == (1 << l) - 1

    got[...] = jnp.zeros_like(got)
    total[...] = jnp.zeros_like(total)
    barrier = pltpu.get_barrier_semaphore()
    for l in range(levels):
        @pl.when(bits[l] == 1)
        def _():
            pl.semaphore_signal(
                barrier, inc=1, device_id={"leaf": sender_of(l)},
                device_id_type=pl.DeviceIdType.MESH,
            )

    wide = x_ref.shape[1]
    b = b_ref[...].astype(F32)
    pad = jnp.zeros((wide - state - 2 * count, rows), F32)
    turned_ref[state:wide, :] = jnp.concatenate([b, b, pad], axis=0).astype(BF16)
    u_copy.wait()
    x_ref[...] = turned_ref[...].T

    edge = state // LANES * LANES
    above = state - edge
    low = lax.broadcasted_iota(jnp.int32, (1, wide), 1) >= state + count

    def multiply(m):
        return dot(d_buf[m * chunk:(m + 1) * chunk, :], x_ref[...])

    def project(m, block):
        at = slice(m * chunk, (m + 1) * chunk)
        tall_ref[at, :] = block[:, edge:edge + LANES]
        high = block.astype(BF16)
        both = jnp.where(low, block - high.astype(F32), block).astype(BF16)
        w_ref[at, :] = both
        return dot(v_buf[:, at], both)

    block = None
    r = jnp.zeros((state, wide), F32)
    for m in range(chunks):
        d_copy(m).wait()
        if m == 1:
            v_copy.wait()
        after = multiply(m)
        if m:
            r = r + project(m - 1, block)
        block = after
    r = (r + project(chunks - 1, block)).T

    lane = lax.broadcasted_iota(jnp.int32, (1, state), 1)
    limit = jnp.zeros((1, state), jnp.int32)
    for l in range(levels):
        limit = jnp.where(lane // rank_top == l, ranks_ref[l], limit)
    r = jnp.where(lane % rank_top < limit, r, 0.0)
    for t in range(tiles):
        wide = min(LANES, state - t * LANES)
        part = r[:, t * LANES:t * LANES + wide]
        total[t, 0:count, 0:wide] = (
            part[state:state + count] + part[state + count:state + 2 * count]
        )
        total[t, count:count + state, 0:wide] = -part[0:state]

    def tile_of(l):
        return l * rank_top // LANES

    def tile_used(l, t):
        used = bits[0] < 0
        for c in range(l + 1, levels):
            if tile_of(c) == t:
                used = jnp.logical_or(used, bits[c] == 0)
        return used

    def row_block(m):
        if m is None:
            return pl.ds(0, count)
        return pl.ds(count + m * rank_top, rank_top)

    def copies(l):
        out = []
        last = (1 << l) - 1
        first = lax.div(me, 2 << l) * (2 << l) + (1 << l)
        for place in range(last, -1, -1):
            for m in [None] + list(range(l + 1, levels)):
                for t in range(tiles):
                    if t != tile_of(l) and (place != last or all(tile_of(c) != t for c in range(l + 1, levels))):
                        continue
                    condition = []
                    if m is not None:
                        condition.append(bits[m] == 1)
                    if t != tile_of(l):
                        condition.append(tile_used(l, t))
                    slot = 0 if m is None else m + 1
                    out.append((place, condition, pltpu.make_async_remote_copy(
                        src_ref=total.at[t, row_block(m), :],
                        dst_ref=got.at[l, t, row_block(m), :],
                        send_sem=send_sem.at[len(out)],
                        recv_sem=got_sem.at[l, t, slot],
                        device_id={"leaf": first + place},
                        device_id_type=pl.DeviceIdType.MESH,
                    )))
        return out

    def guarded(conditions, action):
        if conditions:
            pl.when(functools.reduce(jnp.logical_and, conditions))(action)
        else:
            action()

    def receive(l):
        for place, condition, copy in copies(l):
            if place != (1 << l) - 1:
                continue
            guarded(condition, copy.wait_recv)

    def receive_narrow(l):
        t = tile_of(l)
        for m in [None] + list(range(l + 1, levels)):
            copy = pltpu.make_async_remote_copy(
                src_ref=total.at[t, row_block(m), :],
                dst_ref=got.at[l, t, row_block(m), :],
                send_sem=send_sem.at[0],
                recv_sem=got_sem.at[l, t, 0 if m is None else m + 1],
                device_id={"leaf": sender_of(l)},
                device_id_type=pl.DeviceIdType.MESH,
            )
            guarded([] if m is None else [bits[m] == 1], copy.wait_recv)

    def join(l):
        own = tile_of(l)
        start = l * rank_top - own * LANES
        row = lax.broadcasted_iota(jnp.int32, (LANES, LANES), 0)
        inside = jnp.logical_and(row >= start, row < start + rank_top)

        def update(lo, hi):
            factor = got[l, own, lo:hi, :]
            for t in range(tiles):
                if all(tile_of(c) != t for c in range(l + 1, levels)):
                    continue
                at = count + own * LANES
                step = jnp.where(inside, total[t, at:at + LANES, :], 0.0)
                total[t, lo:hi, :] = (
                    total[t, lo:hi, :] + got[l, t, lo:hi, :] + dot_split(factor, step)
                )

        update(0, count)
        if l + 1 < levels:
            @pl.when(lax.div(me, 2 << l) > 0)
            def _():
                update(count + (l + 1) * rank_top, count + state)

    def absorb(l):
        own = tile_of(l)
        start = l * rank_top - own * LANES
        row = lax.broadcasted_iota(jnp.int32, (LANES, LANES), 0)
        inside = jnp.logical_and(row >= start, row < start + rank_top)

        def update(lo, hi):
            factor = got[l, own, lo:hi, :]
            for c in range(l):
                t = tile_of(c)
                at = count + own * LANES
                step = jnp.where(inside, got[c, t, at:at + LANES, :], 0.0)
                got[c, t, lo:hi, :] = got[c, t, lo:hi, :] + dot_split(factor, step)

        update(0, count)
        if l + 1 < levels:
            @pl.when(lax.div(me, 2 << l) > 0)
            def _():
                update(count + (l + 1) * rank_top, count + state)

    for l in range(levels):
        sends = jnp.logical_and(is_last(l), bits[l] == 0)
        if l:
            takes = jnp.logical_and(is_last(l), bits[l] == 1)
            others = jnp.logical_and(jnp.logical_not(is_last(l)), bits[l] == 1)
        else:
            takes, others = bits[l] == 1, None

        @pl.when(sends)
        def _():
            pl.semaphore_wait(barrier, 1 << l)
            for _, condition, copy in copies(l):
                guarded(condition, copy.start)

        if l == levels - 1:
            c_ref[...] = tall_ref[...].T[above:above + count]
            wt_ref[...] = w_ref[:, 0:state].T

        @pl.when(takes)
        def _():
            receive(l)
            if l + 1 < levels:
                join(l)
            if l:
                absorb(l)

        if others is not None:
            @pl.when(others)
            def _():
                receive_narrow(l)
                absorb(l)

    lane = lax.broadcasted_iota(jnp.int32, (1, LANES), 1)
    parts = [jnp.zeros((count, LANES), F32)] * tiles
    for l in range(levels):
        t = tile_of(l)
        start = l * rank_top - t * LANES
        inside = jnp.logical_and(lane >= start, lane < start + rank_top)
        parts[t] = jnp.where(inside, got[l, t, 0:count, :], parts[t])
    p = jnp.concatenate(parts, axis=1)[:, 0:state]
    high = p.astype(BF16).astype(F32)
    both = jnp.concatenate([high, p - high], axis=0).astype(BF16)
    moved = dot(both, wt_ref[...])
    moved_ref[...] = moved[0:count] + moved[count:2 * count]

    for l in range(levels):
        @pl.when(jnp.logical_and(is_last(l), bits[l] == 0))
        def _():
            for _, condition, copy in copies(l):
                guarded(condition, copy.wait_send)


def on_device(rhs_vectors, diag_inverse, left_factors, right_factors, ranks):
    leaves = lax.axis_size("leaf")
    levels = leaves.bit_length() - 1
    count, rows = rhs_vectors.shape
    state = left_factors.shape[1]
    rank_top = state // levels
    tiles = pl.cdiv(state, LANES)
    chunk = rows // 4
    wide = pl.cdiv(state + 2 * count, LANES) * LANES
    most = 0
    for l in range(levels):
        most = max(most, ((1 << l) - 1 + tiles) * (levels - l))
    vmem = pl.BlockSpec(memory_space=pltpu.VMEM)
    hbm = pl.BlockSpec(memory_space=pltpu.HBM)
    base, moved = pl.pallas_call(
        functools.partial(kernel, levels, rank_top, chunk),
        out_shape=[jax.ShapeDtypeStruct((count, rows), F32)] * 2,
        in_specs=[pl.BlockSpec(memory_space=pltpu.SMEM), vmem, hbm, hbm, hbm],
        out_specs=[vmem, vmem],
        scratch_shapes=[
            pltpu.VMEM(diag_inverse.shape, BF16),
            pltpu.VMEM((state, rows), BF16),
            pltpu.VMEM((wide, rows), BF16),
            pltpu.VMEM((rows, wide), BF16),
            pltpu.VMEM((rows, wide), BF16),
            pltpu.VMEM((rows, LANES), F32),
            pltpu.VMEM((state, rows), BF16),
            pltpu.VMEM((tiles, count + tiles * LANES, LANES), F32),
            pltpu.VMEM((levels, tiles, count + tiles * LANES, LANES), F32),
            pltpu.SemaphoreType.DMA((rows // chunk,)),
            pltpu.SemaphoreType.DMA,
            pltpu.SemaphoreType.DMA,
            pltpu.SemaphoreType.DMA((most,)),
            pltpu.SemaphoreType.DMA((levels, tiles, levels + 1)),
        ],
        compiler_params=pltpu.CompilerParams(
            collective_id=0, has_side_effects=True, vmem_limit_bytes=55040 * 1024
        ),
        cost_estimate=pl.CostEstimate(
            flops=2 * rows * rows * wide, bytes_accessed=2 * rows * (rows + 2 * state), transcendentals=0
        ),
    )(ranks, rhs_vectors, diag_inverse, left_factors.T, right_factors.T)
    return base - moved


def solution(mesh):
    in_specs = (P("rhs", "leaf"), P("leaf", None), P("leaf", None), P("leaf", None), P())
    return jax.shard_map(
        on_device, mesh=mesh, in_specs=in_specs, out_specs=P("rhs", "leaf"), check_vma=False
    )
```

```python
import functools

import jax
import jax.numpy as jnp
from jax import lax
from jax.experimental import pallas as pl
from jax.experimental.pallas import tpu as pltpu
from jax.sharding import PartitionSpec as P

LANES = 128
F32 = jnp.float32
BF16 = jnp.bfloat16


def split(x):
    high = x.astype(BF16)
    return high, (x - high.astype(F32)).astype(BF16)


def dot(a, b):
    return jnp.dot(a, b, preferred_element_type=F32)


def dot_turned(a, b):
    return lax.dot_general(a, b, (((1,), (1,)), ((), ())), preferred_element_type=F32)


def dot_split(a, b):
    a_high, a_low = split(a)
    b_high, b_low = split(b)
    return dot(a_high, b_high) + (dot(a_high, b_low) + dot(a_low, b_high))


def kernel(
    levels, rank_top, chunk,
    ranks_ref, b_ref, d_hbm, u_hbm, v_hbm, c_ref, moved_ref,
    d_buf, v_buf, x_ref, wt_ref, r_ref, total, got,
    d_sem, u_sem, v_sem, send_sem, got_sem,
):
    me = lax.axis_index("leaf")
    rows = d_buf.shape[0]
    chunks = rows // chunk
    state = v_buf.shape[0]
    count = b_ref.shape[0]
    tiles = total.shape[0]
    bits = [lax.rem(lax.div(me, 1 << l), 2) for l in range(levels)]

    pieces = d_sem.shape[0]
    piece = rows // pieces
    flight = 3

    def d_copy(m):
        at = pl.ds(m * piece, piece)
        return pltpu.make_async_copy(d_hbm.at[at, :], d_buf.at[at, :], d_sem.at[m])

    u_copy = pltpu.make_async_copy(u_hbm, x_ref.at[pl.ds(0, state), :], u_sem)
    v_copy = pltpu.make_async_copy(v_hbm, v_buf, v_sem)
    u_copy.start()
    d_copy(0).start()

    def sender_of(l):
        span = 2 << l
        return lax.div(me, span) * span + ((1 << l) - 1)

    def is_last(l):
        return lax.rem(me, 1 << l) == (1 << l) - 1

    got[...] = jnp.zeros_like(got)
    total[...] = jnp.zeros_like(total)
    barrier = pltpu.get_barrier_semaphore()
    for l in range(levels):
        @pl.when(bits[l] == 1)
        def _():
            pl.semaphore_signal(
                barrier, inc=1, device_id={"leaf": sender_of(l)},
                device_id_type=pl.DeviceIdType.MESH,
            )

    b = b_ref[...].astype(F32)
    x_ref[state:state + 2 * count, :] = jnp.concatenate([b, b], axis=0).astype(BF16)
    u_copy.wait()
    for m in range(1, flight):
        d_copy(m).start()
    r_ref[...] = jnp.zeros_like(r_ref)

    def multiply(m):
        at = pl.ds(m * chunk, chunk)
        return dot_turned(x_ref[...], d_buf[at, :])

    def project(m, block):
        at = pl.ds(m * chunk, chunk)
        w = block[0:state].astype(BF16)
        twice = block[state:state + 2 * count]
        c_ref[:, at] = twice[0:count]
        high = twice.astype(BF16).astype(F32)
        row = lax.broadcasted_iota(jnp.int32, twice.shape, 0)
        both = jnp.where(row < count, high, twice - high).astype(BF16)
        wt_ref[:, at] = w
        r_ref[...] += dot_turned(jnp.concatenate([w, both], axis=0), v_buf[:, at])

    block = None
    per = chunk // piece
    for m in range(chunks):
        for part in range(m * per, (m + 1) * per):
            d_copy(part).wait()
            if part + flight < pieces:
                d_copy(part + flight).start()
            if part == 0:
                v_copy.start()
        if m == 1:
            v_copy.wait()
        after = multiply(m)
        if m:
            project(m - 1, block)
        block = after
    project(chunks - 1, block)

    lane = lax.broadcasted_iota(jnp.int32, (1, state), 1)
    limit = jnp.zeros((1, state), jnp.int32)
    for l in range(levels):
        limit = jnp.where(lane // rank_top == l, ranks_ref[l], limit)
    r = jnp.where(lane % rank_top < limit, r_ref[...], 0.0)
    for t in range(tiles):
        wide = min(LANES, state - t * LANES)
        part = r[:, t * LANES:t * LANES + wide]
        total[t, 0:count, 0:wide] = (
            part[state:state + count] + part[state + count:state + 2 * count]
        )
        total[t, count:count + state, 0:wide] = -part[0:state]

    def tile_of(l):
        return l * rank_top // LANES

    def tile_used(l, t):
        used = bits[0] < 0
        for c in range(l + 1, levels):
            if tile_of(c) == t:
                used = jnp.logical_or(used, bits[c] == 0)
        return used

    def row_block(m):
        if m is None:
            return pl.ds(0, count)
        return pl.ds(count + m * rank_top, rank_top)

    def copies(l):
        out = []
        last = (1 << l) - 1
        first = lax.div(me, 2 << l) * (2 << l) + (1 << l)
        for place in range(last, -1, -1):
            for m in [None] + list(range(l + 1, levels)):
                for t in range(tiles):
                    if t != tile_of(l) and (place != last or all(tile_of(c) != t for c in range(l + 1, levels))):
                        continue
                    condition = []
                    if m is not None:
                        condition.append(bits[m] == 1)
                    if t != tile_of(l):
                        condition.append(tile_used(l, t))
                    slot = 0 if m is None else m + 1
                    out.append((place, condition, pltpu.make_async_remote_copy(
                        src_ref=total.at[t, row_block(m), :],
                        dst_ref=got.at[l, t, row_block(m), :],
                        send_sem=send_sem.at[len(out)],
                        recv_sem=got_sem.at[l, t, slot],
                        device_id={"leaf": first + place},
                        device_id_type=pl.DeviceIdType.MESH,
                    )))
        return out

    def guarded(conditions, action):
        if conditions:
            pl.when(functools.reduce(jnp.logical_and, conditions))(action)
        else:
            action()

    def receive(l):
        for place, condition, copy in copies(l):
            if place != (1 << l) - 1:
                continue
            guarded(condition, copy.wait_recv)

    def receive_narrow(l):
        t = tile_of(l)
        for m in [None] + list(range(l + 1, levels)):
            copy = pltpu.make_async_remote_copy(
                src_ref=total.at[t, row_block(m), :],
                dst_ref=got.at[l, t, row_block(m), :],
                send_sem=send_sem.at[0],
                recv_sem=got_sem.at[l, t, 0 if m is None else m + 1],
                device_id={"leaf": sender_of(l)},
                device_id_type=pl.DeviceIdType.MESH,
            )
            guarded([] if m is None else [bits[m] == 1], copy.wait_recv)

    def join(l):
        own = tile_of(l)
        start = l * rank_top - own * LANES
        row = lax.broadcasted_iota(jnp.int32, (LANES, LANES), 0)
        inside = jnp.logical_and(row >= start, row < start + rank_top)

        def update(lo, hi):
            factor = got[l, own, lo:hi, :]
            for t in range(tiles):
                if all(tile_of(c) != t for c in range(l + 1, levels)):
                    continue
                at = count + own * LANES
                step = jnp.where(inside, total[t, at:at + LANES, :], 0.0)
                total[t, lo:hi, :] = (
                    total[t, lo:hi, :] + got[l, t, lo:hi, :] + dot_split(factor, step)
                )

        update(0, count)
        if l + 1 < levels:
            @pl.when(lax.div(me, 2 << l) > 0)
            def _():
                update(count + (l + 1) * rank_top, count + state)

    def absorb(l):
        own = tile_of(l)
        start = l * rank_top - own * LANES
        row = lax.broadcasted_iota(jnp.int32, (LANES, LANES), 0)
        inside = jnp.logical_and(row >= start, row < start + rank_top)

        def update(lo, hi):
            factor = got[l, own, lo:hi, :]
            for c in range(l):
                t = tile_of(c)
                at = count + own * LANES
                step = jnp.where(inside, got[c, t, at:at + LANES, :], 0.0)
                got[c, t, lo:hi, :] = got[c, t, lo:hi, :] + dot_split(factor, step)

        update(0, count)
        if l + 1 < levels:
            @pl.when(lax.div(me, 2 << l) > 0)
            def _():
                update(count + (l + 1) * rank_top, count + state)

    for l in range(levels):
        sends = jnp.logical_and(is_last(l), bits[l] == 0)
        if l:
            takes = jnp.logical_and(is_last(l), bits[l] == 1)
            others = jnp.logical_and(jnp.logical_not(is_last(l)), bits[l] == 1)
        else:
            takes, others = bits[l] == 1, None

        @pl.when(sends)
        def _():
            pl.semaphore_wait(barrier, 1 << l)
            for _, condition, copy in copies(l):
                guarded(condition, copy.start)

        @pl.when(takes)
        def _():
            receive(l)
            if l + 1 < levels:
                join(l)
            if l:
                absorb(l)

        if others is not None:
            @pl.when(others)
            def _():
                receive_narrow(l)
                absorb(l)

    lane = lax.broadcasted_iota(jnp.int32, (1, LANES), 1)
    parts = [jnp.zeros((count, LANES), F32)] * tiles
    for l in range(levels):
        t = tile_of(l)
        start = l * rank_top - t * LANES
        inside = jnp.logical_and(lane >= start, lane < start + rank_top)
        parts[t] = jnp.where(inside, got[l, t, 0:count, :], parts[t])
    p = jnp.concatenate(parts, axis=1)[:, 0:state]
    high = p.astype(BF16).astype(F32)
    both = jnp.concatenate([high, p - high], axis=0).astype(BF16)
    moved = dot(both, wt_ref[...])
    moved_ref[...] = moved[0:count] + moved[count:2 * count]

    for l in range(levels):
        @pl.when(jnp.logical_and(is_last(l), bits[l] == 0))
        def _():
            for _, condition, copy in copies(l):
                guarded(condition, copy.wait_send)


def on_device(rhs_vectors, diag_inverse, left_factors, right_factors, ranks):
    leaves = lax.axis_size("leaf")
    levels = leaves.bit_length() - 1
    count, rows = rhs_vectors.shape
    state = left_factors.shape[1]
    rank_top = state // levels
    tiles = pl.cdiv(state, LANES)
    chunk = rows // 4
    most = 0
    for l in range(levels):
        most = max(most, ((1 << l) - 1 + tiles) * (levels - l))
    vmem = pl.BlockSpec(memory_space=pltpu.VMEM)
    hbm = pl.BlockSpec(memory_space=pltpu.HBM)
    base, moved = pl.pallas_call(
        functools.partial(kernel, levels, rank_top, chunk),
        out_shape=[jax.ShapeDtypeStruct((count, rows), F32)] * 2,
        in_specs=[pl.BlockSpec(memory_space=pltpu.SMEM), vmem, hbm, hbm, hbm],
        out_specs=[vmem, vmem],
        scratch_shapes=[
            pltpu.VMEM(diag_inverse.shape, BF16),
            pltpu.VMEM((state, rows), BF16),
            pltpu.VMEM((state + 2 * count, rows), BF16),
            pltpu.VMEM((state, rows), BF16),
            pltpu.VMEM((state + 2 * count, state), F32),
            pltpu.VMEM((tiles, count + tiles * LANES, LANES), F32),
            pltpu.VMEM((levels, tiles, count + tiles * LANES, LANES), F32),
            pltpu.SemaphoreType.DMA((8,)),
            pltpu.SemaphoreType.DMA,
            pltpu.SemaphoreType.DMA,
            pltpu.SemaphoreType.DMA((most,)),
            pltpu.SemaphoreType.DMA((levels, tiles, levels + 1)),
        ],
        compiler_params=pltpu.CompilerParams(
            collective_id=0, has_side_effects=True, vmem_limit_bytes=55040 * 1024
        ),
        cost_estimate=pl.CostEstimate(
            flops=2 * rows * rows * (state + count), bytes_accessed=2 * rows * (rows + 2 * state), transcendentals=0
        ),
    )(ranks, rhs_vectors, diag_inverse, left_factors.T, right_factors.T)
    return base - moved


def solution(mesh):
    in_specs = (P("rhs", "leaf"), P("leaf", None), P("leaf", None), P("leaf", None), P())
    return jax.shard_map(
        on_device, mesh=mesh, in_specs=in_specs, out_specs=P("rhs", "leaf"), check_vma=False
    )
```

```python
import functools

import jax
import jax.numpy as jnp
from jax import lax
from jax.experimental import pallas as pl
from jax.experimental.pallas import tpu as pltpu
from jax.sharding import PartitionSpec as P

LANES = 128
F32 = jnp.float32
BF16 = jnp.bfloat16


def split(x):
    high = x.astype(BF16)
    return high, (x - high.astype(F32)).astype(BF16)


def dot(a, b):
    return jnp.dot(a, b, preferred_element_type=F32)


def dot_turned(a, b):
    return lax.dot_general(a, b, (((1,), (1,)), ((), ())), preferred_element_type=F32)


def dot_split(a, b):
    a_high, a_low = split(a)
    b_high, b_low = split(b)
    return dot(a_high, b_high) + (dot(a_high, b_low) + dot(a_low, b_high))


def kernel(
    levels, rank_top, chunk,
    ranks_ref, b_ref, d_hbm, u_hbm, v_hbm, c_ref, moved_ref,
    d_buf, v_buf, x_ref, wt_ref, r_ref, total, got,
    d_sem, u_sem, v_sem, send_sem, got_sem,
):
    me = lax.axis_index("leaf")
    rows = d_buf.shape[0]
    chunks = rows // chunk
    state = v_buf.shape[0]
    count = b_ref.shape[0]
    tiles = total.shape[0]
    bits = [lax.rem(lax.div(me, 1 << l), 2) for l in range(levels)]

    pieces = d_sem.shape[0]
    piece = rows // pieces
    flight = 3

    def d_copy(m):
        at = pl.ds(m * piece, piece)
        return pltpu.make_async_copy(d_hbm.at[at, :], d_buf.at[at, :], d_sem.at[m])

    u_copy = pltpu.make_async_copy(u_hbm, x_ref.at[pl.ds(0, state), :], u_sem)
    v_copy = pltpu.make_async_copy(v_hbm, v_buf, v_sem)
    u_copy.start()
    for m in range(flight):
        d_copy(m).start()

    def sender_of(l):
        span = 2 << l
        return lax.div(me, span) * span + ((1 << l) - 1)

    def is_last(l):
        return lax.rem(me, 1 << l) == (1 << l) - 1

    got[...] = jnp.zeros_like(got)
    total[...] = jnp.zeros_like(total)
    barrier = pltpu.get_barrier_semaphore()
    for l in range(levels):
        @pl.when(bits[l] == 1)
        def _():
            pl.semaphore_signal(
                barrier, inc=1, device_id={"leaf": sender_of(l)},
                device_id_type=pl.DeviceIdType.MESH,
            )

    b = b_ref[...].astype(F32)
    x_ref[state:state + 2 * count, :] = jnp.concatenate([b, b], axis=0).astype(BF16)
    u_copy.wait()
    r_ref[...] = jnp.zeros_like(r_ref)

    def multiply(m):
        at = pl.ds(m * chunk, chunk)
        return dot_turned(x_ref[...], d_buf[at, :])

    def project(m, block):
        at = pl.ds(m * chunk, chunk)
        w = block[0:state].astype(BF16)
        twice = block[state:state + 2 * count]
        c_ref[:, at] = twice[0:count]
        high = twice.astype(BF16).astype(F32)
        row = lax.broadcasted_iota(jnp.int32, twice.shape, 0)
        both = jnp.where(row < count, high, twice - high).astype(BF16)
        wt_ref[:, at] = w
        r_ref[...] += dot_turned(jnp.concatenate([w, both], axis=0), v_buf[:, at])

    block = None
    per = chunk // piece
    for m in range(chunks):
        for part in range(m * per, (m + 1) * per):
            d_copy(part).wait()
            if part + flight < pieces:
                d_copy(part + flight).start()
            if part == 0:
                v_copy.start()
        if m == 1:
            v_copy.wait()
        after = multiply(m)
        if m:
            project(m - 1, block)
        block = after
    project(chunks - 1, block)

    lane = lax.broadcasted_iota(jnp.int32, (1, state), 1)
    limit = jnp.zeros((1, state), jnp.int32)
    for l in range(levels):
        limit = jnp.where(lane // rank_top == l, ranks_ref[l], limit)
    r = jnp.where(lane % rank_top < limit, r_ref[...], 0.0)
    for t in range(tiles):
        wide = min(LANES, state - t * LANES)
        part = r[:, t * LANES:t * LANES + wide]
        total[t, 0:count, 0:wide] = (
            part[state:state + count] + part[state + count:state + 2 * count]
        )
        total[t, count:count + state, 0:wide] = -part[0:state]

    def tile_of(l):
        return l * rank_top // LANES

    def tile_used(l, t):
        used = bits[0] < 0
        for c in range(l + 1, levels):
            if tile_of(c) == t:
                used = jnp.logical_or(used, bits[c] == 0)
        return used

    def row_block(m):
        if m is None:
            return pl.ds(0, count)
        return pl.ds(count + m * rank_top, rank_top)

    def copies(l):
        out = []
        last = (1 << l) - 1
        first = lax.div(me, 2 << l) * (2 << l) + (1 << l)
        for place in range(last, -1, -1):
            for m in [None] + list(range(l + 1, levels)):
                for t in range(tiles):
                    if t != tile_of(l) and (place != last or all(tile_of(c) != t for c in range(l + 1, levels))):
                        continue
                    condition = []
                    if m is not None:
                        condition.append(bits[m] == 1)
                    if t != tile_of(l):
                        condition.append(tile_used(l, t))
                    slot = 0 if m is None else m + 1
                    out.append((place, condition, pltpu.make_async_remote_copy(
                        src_ref=total.at[t, row_block(m), :],
                        dst_ref=got.at[l, t, row_block(m), :],
                        send_sem=send_sem.at[len(out)],
                        recv_sem=got_sem.at[l, t, slot],
                        device_id={"leaf": first + place},
                        device_id_type=pl.DeviceIdType.MESH,
                    )))
        return out

    def guarded(conditions, action):
        if conditions:
            pl.when(functools.reduce(jnp.logical_and, conditions))(action)
        else:
            action()

    def receive(l):
        for place, condition, copy in copies(l):
            if place != (1 << l) - 1:
                continue
            guarded(condition, copy.wait_recv)

    def receive_narrow(l):
        t = tile_of(l)
        for m in [None] + list(range(l + 1, levels)):
            copy = pltpu.make_async_remote_copy(
                src_ref=total.at[t, row_block(m), :],
                dst_ref=got.at[l, t, row_block(m), :],
                send_sem=send_sem.at[0],
                recv_sem=got_sem.at[l, t, 0 if m is None else m + 1],
                device_id={"leaf": sender_of(l)},
                device_id_type=pl.DeviceIdType.MESH,
            )
            guarded([] if m is None else [bits[m] == 1], copy.wait_recv)

    def join(l):
        own = tile_of(l)
        start = l * rank_top - own * LANES
        row = lax.broadcasted_iota(jnp.int32, (LANES, LANES), 0)
        inside = jnp.logical_and(row >= start, row < start + rank_top)

        def update(lo, hi):
            factor = got[l, own, lo:hi, :]
            for t in range(tiles):
                if all(tile_of(c) != t for c in range(l + 1, levels)):
                    continue
                at = count + own * LANES
                step = jnp.where(inside, total[t, at:at + LANES, :], 0.0)
                total[t, lo:hi, :] = (
                    total[t, lo:hi, :] + got[l, t, lo:hi, :] + dot_split(factor, step)
                )

        update(0, count)
        if l + 1 < levels:
            @pl.when(lax.div(me, 2 << l) > 0)
            def _():
                update(count + (l + 1) * rank_top, count + state)

    def absorb(l):
        own = tile_of(l)
        start = l * rank_top - own * LANES
        row = lax.broadcasted_iota(jnp.int32, (LANES, LANES), 0)
        inside = jnp.logical_and(row >= start, row < start + rank_top)

        def update(lo, hi):
            factor = got[l, own, lo:hi, :]
            for c in range(l):
                t = tile_of(c)
                at = count + own * LANES
                step = jnp.where(inside, got[c, t, at:at + LANES, :], 0.0)
                got[c, t, lo:hi, :] = got[c, t, lo:hi, :] + dot_split(factor, step)

        update(0, count)
        if l + 1 < levels:
            @pl.when(lax.div(me, 2 << l) > 0)
            def _():
                update(count + (l + 1) * rank_top, count + state)

    for l in range(levels):
        sends = jnp.logical_and(is_last(l), bits[l] == 0)
        if l:
            takes = jnp.logical_and(is_last(l), bits[l] == 1)
            others = jnp.logical_and(jnp.logical_not(is_last(l)), bits[l] == 1)
        else:
            takes, others = bits[l] == 1, None

        @pl.when(sends)
        def _():
            pl.semaphore_wait(barrier, 1 << l)
            for _, condition, copy in copies(l):
                guarded(condition, copy.start)

        if l > 1:
            pl.when(bits[l - 1] == 1)(functools.partial(absorb, l - 1))

        @pl.when(takes)
        def _():
            receive(l)
            if l + 1 < levels:
                join(l)

        if others is not None:
            @pl.when(others)
            def _():
                receive_narrow(l)

    pl.when(bits[levels - 1] == 1)(functools.partial(absorb, levels - 1))

    lane = lax.broadcasted_iota(jnp.int32, (1, LANES), 1)
    parts = [jnp.zeros((count, LANES), F32)] * tiles
    for l in range(levels):
        t = tile_of(l)
        start = l * rank_top - t * LANES
        inside = jnp.logical_and(lane >= start, lane < start + rank_top)
        parts[t] = jnp.where(inside, got[l, t, 0:count, :], parts[t])
    p = jnp.concatenate(parts, axis=1)[:, 0:state]
    high = p.astype(BF16).astype(F32)
    both = jnp.concatenate([high, p - high], axis=0).astype(BF16)
    moved = dot(both, wt_ref[...])
    moved_ref[...] = moved[0:count] + moved[count:2 * count]

    for l in range(levels):
        @pl.when(jnp.logical_and(is_last(l), bits[l] == 0))
        def _():
            for _, condition, copy in copies(l):
                guarded(condition, copy.wait_send)


def on_device(rhs_vectors, diag_inverse, left_factors, right_factors, ranks):
    leaves = lax.axis_size("leaf")
    levels = leaves.bit_length() - 1
    count, rows = rhs_vectors.shape
    state = left_factors.shape[1]
    rank_top = state // levels
    tiles = pl.cdiv(state, LANES)
    chunk = rows // 4
    most = 0
    for l in range(levels):
        most = max(most, ((1 << l) - 1 + tiles) * (levels - l))
    vmem = pl.BlockSpec(memory_space=pltpu.VMEM)
    hbm = pl.BlockSpec(memory_space=pltpu.HBM)
    base, moved = pl.pallas_call(
        functools.partial(kernel, levels, rank_top, chunk),
        out_shape=[jax.ShapeDtypeStruct((count, rows), F32)] * 2,
        in_specs=[pl.BlockSpec(memory_space=pltpu.SMEM), vmem, hbm, hbm, hbm],
        out_specs=[vmem, vmem],
        scratch_shapes=[
            pltpu.VMEM(diag_inverse.shape, BF16),
            pltpu.VMEM((state, rows), BF16),
            pltpu.VMEM((state + 2 * count, rows), BF16),
            pltpu.VMEM((state, rows), BF16),
            pltpu.VMEM((state + 2 * count, state), F32),
            pltpu.VMEM((tiles, count + tiles * LANES, LANES), F32),
            pltpu.VMEM((levels, tiles, count + tiles * LANES, LANES), F32),
            pltpu.SemaphoreType.DMA((8,)),
            pltpu.SemaphoreType.DMA,
            pltpu.SemaphoreType.DMA,
            pltpu.SemaphoreType.DMA((most,)),
            pltpu.SemaphoreType.DMA((levels, tiles, levels + 1)),
        ],
        compiler_params=pltpu.CompilerParams(
            collective_id=0, has_side_effects=True, vmem_limit_bytes=55040 * 1024
        ),
        cost_estimate=pl.CostEstimate(
            flops=2 * rows * rows * (state + count), bytes_accessed=2 * rows * (rows + 2 * state), transcendentals=0
        ),
    )(ranks, rhs_vectors, diag_inverse, left_factors.T, right_factors.T)
    return base - moved


def solution(mesh):
    in_specs = (P("rhs", "leaf"), P("leaf", None), P("leaf", None), P("leaf", None), P())
    return jax.shard_map(
        on_device, mesh=mesh, in_specs=in_specs, out_specs=P("rhs", "leaf"), check_vma=False
    )
```

```python
import functools

import jax
import jax.numpy as jnp
from jax import lax
from jax.experimental import pallas as pl
from jax.experimental.pallas import tpu as pltpu
from jax.sharding import PartitionSpec as P

LANES = 128
F32 = jnp.float32
BF16 = jnp.bfloat16


def split(x):
    high = x.astype(BF16)
    return high, (x - high.astype(F32)).astype(BF16)


def dot(a, b):
    return jnp.dot(a, b, preferred_element_type=F32)


def dot_turned(a, b):
    return lax.dot_general(a, b, (((1,), (1,)), ((), ())), preferred_element_type=F32)


def dot_split(a, b):
    n = a.shape[0]
    high = a.astype(BF16).astype(F32)
    both = jnp.concatenate([high, a - high], axis=0).astype(BF16)
    whole = dot(both, b[0]) + dot(both, b[1])
    return whole[0:n] + whole[n:2 * n]


def kernel(
    levels, rank_top,
    ranks_ref, b_ref, d_hbm, u_hbm, v_hbm, c_ref, moved_ref,
    d_buf, v_buf, x_ref, wt_ref, r_ref, total, got,
    d_sem, u_sem, v_sem, send_sem, got_sem,
):
    me = lax.axis_index("leaf")
    rows = d_buf.shape[0]
    state = v_buf.shape[0]
    count = b_ref.shape[0]
    tiles = total.shape[0]
    bits = [lax.rem(lax.div(me, 1 << l), 2) for l in range(levels)]

    pieces = d_sem.shape[0]
    piece = rows // pieces
    flight = 3

    def d_copy(m):
        at = pl.ds(m * piece, piece)
        return pltpu.make_async_copy(d_hbm.at[at, :], d_buf.at[at, :], d_sem.at[m])

    u_copy = pltpu.make_async_copy(u_hbm, x_ref.at[pl.ds(0, state), :], u_sem)
    v_copy = pltpu.make_async_copy(v_hbm, v_buf, v_sem)
    u_copy.start()
    for m in range(flight):
        d_copy(m).start()

    def sender_of(l):
        span = 2 << l
        return lax.div(me, span) * span + ((1 << l) - 1)

    def is_last(l):
        return lax.rem(me, 1 << l) == (1 << l) - 1

    got[...] = jnp.zeros_like(got)
    total[...] = jnp.zeros_like(total)
    barrier = pltpu.get_barrier_semaphore()
    for l in range(levels):
        @pl.when(bits[l] == 1)
        def _():
            pl.semaphore_signal(
                barrier, inc=1, device_id={"leaf": sender_of(l)},
                device_id_type=pl.DeviceIdType.MESH,
            )

    b = b_ref[...].astype(F32)
    x_ref[state:state + 2 * count, :] = jnp.concatenate([b, b], axis=0).astype(BF16)
    u_copy.wait()
    r_ref[...] = jnp.zeros_like(r_ref)

    def multiply(at):
        return dot_turned(x_ref[...], d_buf[at, :])

    def project(at, block):
        w = block[0:state].astype(BF16)
        twice = block[state:state + 2 * count]
        c_ref[:, at] = twice[0:count]
        high = twice.astype(BF16).astype(F32)
        row = lax.broadcasted_iota(jnp.int32, twice.shape, 0)
        both = jnp.where(row < count, high, twice - high).astype(BF16)
        wt_ref[:, at] = w
        r_ref[...] += dot_turned(jnp.concatenate([w, both], axis=0), v_buf[:, at])

    block, before = None, None
    for first, last in ((0, 2), (2, 4), (4, 6), (6, 7), (7, 8)):
        for part in range(first, last):
            d_copy(part).wait()
            if part + flight < pieces:
                d_copy(part + flight).start()
            if part == 0:
                v_copy.start()
        if first == 2:
            v_copy.wait()
        at = pl.ds(first * piece, (last - first) * piece)
        after = multiply(at)
        if before is not None:
            project(before, block)
        block, before = after, at
    project(before, block)

    lane = lax.broadcasted_iota(jnp.int32, (1, state), 1)
    limit = jnp.zeros((1, state), jnp.int32)
    for l in range(levels):
        limit = jnp.where(lane // rank_top == l, ranks_ref[l], limit)
    r = jnp.where(lane % rank_top < limit, r_ref[...], 0.0)
    for t in range(tiles):
        wide = min(LANES, state - t * LANES)
        part = r[:, t * LANES:t * LANES + wide]
        total[t, 0:count, 0:wide] = (
            part[state:state + count] + part[state + count:state + 2 * count]
        )
        total[t, count:count + state, 0:wide] = -part[0:state]

    def tile_of(l):
        return l * rank_top // LANES

    def tile_used(l, t):
        used = bits[0] < 0
        for c in range(l + 1, levels):
            if tile_of(c) == t:
                used = jnp.logical_or(used, bits[c] == 0)
        return used

    def row_block(m):
        if m is None:
            return pl.ds(0, count)
        return pl.ds(count + m * rank_top, rank_top)

    def copies(l):
        out = []
        last = (1 << l) - 1
        first = lax.div(me, 2 << l) * (2 << l) + (1 << l)
        for place in range(last, -1, -1):
            for m in [None] + list(range(l + 1, levels)):
                for t in range(tiles):
                    if t != tile_of(l) and (place != last or all(tile_of(c) != t for c in range(l + 1, levels))):
                        continue
                    condition = []
                    if m is not None:
                        condition.append(bits[m] == 1)
                    if t != tile_of(l):
                        condition.append(tile_used(l, t))
                    slot = 0 if m is None else m + 1
                    out.append((place, condition, pltpu.make_async_remote_copy(
                        src_ref=total.at[t, row_block(m), :],
                        dst_ref=got.at[l, t, row_block(m), :],
                        send_sem=send_sem.at[len(out)],
                        recv_sem=got_sem.at[l, t, slot],
                        device_id={"leaf": first + place},
                        device_id_type=pl.DeviceIdType.MESH,
                    )))
        return out

    def guarded(conditions, action):
        if conditions:
            pl.when(functools.reduce(jnp.logical_and, conditions))(action)
        else:
            action()

    def receive(l):
        for place, condition, copy in copies(l):
            if place != (1 << l) - 1:
                continue
            guarded(condition, copy.wait_recv)

    def receive_narrow(l):
        t = tile_of(l)
        for m in [None] + list(range(l + 1, levels)):
            copy = pltpu.make_async_remote_copy(
                src_ref=total.at[t, row_block(m), :],
                dst_ref=got.at[l, t, row_block(m), :],
                send_sem=send_sem.at[0],
                recv_sem=got_sem.at[l, t, 0 if m is None else m + 1],
                device_id={"leaf": sender_of(l)},
                device_id_type=pl.DeviceIdType.MESH,
            )
            guarded([] if m is None else [bits[m] == 1], copy.wait_recv)

    def level_rows(l, sources):
        own = tile_of(l)
        start = l * rank_top - own * LANES
        row = lax.broadcasted_iota(jnp.int32, (LANES, LANES), 0)
        inside = jnp.logical_and(row >= start, row < start + rank_top)
        at = slice(count + own * LANES, count + (own + 1) * LANES)
        parts = [jnp.where(inside, ref[at, :], 0.0) for ref in sources]
        return split(jnp.concatenate(parts, axis=1))

    def for_rows(l, update):
        update(slice(0, count))
        if l + 1 < levels:
            @pl.when(lax.div(me, 2 << l) > 0)
            def _():
                update(slice(count + (l + 1) * rank_top, count + state))

    def tiles_above(l):
        return sorted({tile_of(c) for c in range(l + 1, levels)})

    def join(l, factors):
        def update(at):
            step = dot_split(got[l, tile_of(l), at, :], factors)
            for place, t in enumerate(tiles_above(l)):
                mine = step[:, place * LANES:(place + 1) * LANES]
                total[t, at, :] = total[t, at, :] + got[l, t, at, :] + mine

        for_rows(l, update)

    def absorb(l, factors):
        def update(at):
            step = dot_split(got[l, tile_of(l), at, :], factors)
            for c in range(l):
                t = tile_of(c)
                got[c, t, at, :] = got[c, t, at, :] + step[:, c * LANES:(c + 1) * LANES]

        for_rows(l, update)

    def below(l):
        return level_rows(l, [got.at[c, tile_of(c)] for c in range(l)])

    for l in range(levels):
        sends = jnp.logical_and(is_last(l), bits[l] == 0)
        if l:
            takes = jnp.logical_and(is_last(l), bits[l] == 1)
            others = jnp.logical_and(jnp.logical_not(is_last(l)), bits[l] == 1)
        else:
            takes, others = bits[l] == 1, None

        @pl.when(sends)
        def _():
            pl.semaphore_wait(barrier, 1 << l)
            for _, condition, copy in copies(l):
                guarded(condition, copy.start)

        if l > 1:
            @pl.when(bits[l - 1] == 1)
            def _():
                absorb(l - 1, below(l - 1))

        if l == levels - 1:
            @pl.when(bits[l] == 1)
            def _():
                factors = below(l) if l else None
                receive_narrow(l)
                if l:
                    absorb(l, factors)

            continue

        @pl.when(takes)
        def _():
            factors = level_rows(l, [total.at[t] for t in tiles_above(l)])
            receive(l)
            join(l, factors)

        if others is not None:
            @pl.when(others)
            def _():
                receive_narrow(l)

    lane = lax.broadcasted_iota(jnp.int32, (1, LANES), 1)
    parts = [jnp.zeros((count, LANES), F32)] * tiles
    for l in range(levels):
        t = tile_of(l)
        start = l * rank_top - t * LANES
        inside = jnp.logical_and(lane >= start, lane < start + rank_top)
        parts[t] = jnp.where(inside, got[l, t, 0:count, :], parts[t])
    p = jnp.concatenate(parts, axis=1)[:, 0:state]
    high = p.astype(BF16).astype(F32)
    both = jnp.concatenate([high, p - high], axis=0).astype(BF16)
    moved = dot(both, wt_ref[...])
    moved_ref[...] = moved[0:count] + moved[count:2 * count]

    for l in range(levels):
        @pl.when(jnp.logical_and(is_last(l), bits[l] == 0))
        def _():
            for _, condition, copy in copies(l):
                guarded(condition, copy.wait_send)


def on_device(rhs_vectors, diag_inverse, left_factors, right_factors, ranks):
    leaves = lax.axis_size("leaf")
    levels = leaves.bit_length() - 1
    count, rows = rhs_vectors.shape
    state = left_factors.shape[1]
    rank_top = state // levels
    tiles = pl.cdiv(state, LANES)
    most = 0
    for l in range(levels):
        most = max(most, ((1 << l) - 1 + tiles) * (levels - l))
    vmem = pl.BlockSpec(memory_space=pltpu.VMEM)
    hbm = pl.BlockSpec(memory_space=pltpu.HBM)
    base, moved = pl.pallas_call(
        functools.partial(kernel, levels, rank_top),
        out_shape=[jax.ShapeDtypeStruct((count, rows), F32)] * 2,
        in_specs=[pl.BlockSpec(memory_space=pltpu.SMEM), vmem, hbm, hbm, hbm],
        out_specs=[vmem, vmem],
        scratch_shapes=[
            pltpu.VMEM(diag_inverse.shape, BF16),
            pltpu.VMEM((state, rows), BF16),
            pltpu.VMEM((state + 2 * count, rows), BF16),
            pltpu.VMEM((state, rows), BF16),
            pltpu.VMEM((state + 2 * count, state), F32),
            pltpu.VMEM((tiles, count + tiles * LANES, LANES), F32),
            pltpu.VMEM((levels, tiles, count + tiles * LANES, LANES), F32),
            pltpu.SemaphoreType.DMA((8,)),
            pltpu.SemaphoreType.DMA,
            pltpu.SemaphoreType.DMA,
            pltpu.SemaphoreType.DMA((most,)),
            pltpu.SemaphoreType.DMA((levels, tiles, levels + 1)),
        ],
        compiler_params=pltpu.CompilerParams(
            collective_id=0, has_side_effects=True, vmem_limit_bytes=55040 * 1024
        ),
        cost_estimate=pl.CostEstimate(
            flops=2 * rows * rows * (state + count), bytes_accessed=2 * rows * (rows + 2 * state), transcendentals=0
        ),
    )(ranks, rhs_vectors, diag_inverse, left_factors.T, right_factors.T)
    return base - moved


def solution(mesh):
    in_specs = (P("rhs", "leaf"), P("leaf", None), P("leaf", None), P("leaf", None), P())
    return jax.shard_map(
        on_device, mesh=mesh, in_specs=in_specs, out_specs=P("rhs", "leaf"), check_vma=False
    )
```

```python
import functools

import jax
import jax.numpy as jnp
from jax import lax
from jax.experimental import pallas as pl
from jax.experimental.pallas import tpu as pltpu
from jax.sharding import PartitionSpec as P

LANES = 128
F32 = jnp.float32
BF16 = jnp.bfloat16


def split(x):
    high = x.astype(BF16)
    return high, (x - high.astype(F32)).astype(BF16)


def dot(a, b):
    return jnp.dot(a, b, preferred_element_type=F32)


def dot_turned(a, b):
    return lax.dot_general(a, b, (((1,), (1,)), ((), ())), preferred_element_type=F32)


def dot_split(a, b):
    n = a.shape[0]
    high = a.astype(BF16).astype(F32)
    both = jnp.concatenate([high, a - high], axis=0).astype(BF16)
    whole = dot(both, b[0]) + dot(both, b[1])
    return whole[0:n] + whole[n:2 * n]


def kernel(
    levels, rank_top,
    ranks_ref, block_ref, v_ref, c_ref, moved_ref,
    wt_ref, total, got, send_sem, got_sem,
):
    me = lax.axis_index("leaf")
    state, rows = v_ref.shape
    count = c_ref.shape[0]
    tiles = total.shape[0]
    bits = [lax.rem(lax.div(me, 1 << l), 2) for l in range(levels)]

    def sender_of(l):
        span = 2 << l
        return lax.div(me, span) * span + ((1 << l) - 1)

    def is_last(l):
        return lax.rem(me, 1 << l) == (1 << l) - 1

    got[...] = jnp.zeros_like(got)
    total[...] = jnp.zeros_like(total)
    barrier = pltpu.get_barrier_semaphore()
    for l in range(levels):
        @pl.when(bits[l] == 1)
        def _():
            pl.semaphore_signal(
                barrier, inc=1, device_id={"leaf": sender_of(l)},
                device_id_type=pl.DeviceIdType.MESH,
            )

    w = block_ref[0:state, :].astype(BF16)
    wt_ref[...] = w
    twice = block_ref[state:state + 2 * count, :]
    c_ref[...] = twice[0:count]
    high = twice.astype(BF16).astype(F32)
    row = lax.broadcasted_iota(jnp.int32, twice.shape, 0)
    both = jnp.where(row < count, high, twice - high).astype(BF16)
    r = dot_turned(jnp.concatenate([w, both], axis=0), v_ref[...])

    lane = lax.broadcasted_iota(jnp.int32, (1, state), 1)
    limit = jnp.zeros((1, state), jnp.int32)
    for l in range(levels):
        limit = jnp.where(lane // rank_top == l, ranks_ref[l], limit)
    r = jnp.where(lane % rank_top < limit, r, 0.0)
    for t in range(tiles):
        wide = min(LANES, state - t * LANES)
        part = r[:, t * LANES:t * LANES + wide]
        total[t, 0:count, 0:wide] = (
            part[state:state + count] + part[state + count:state + 2 * count]
        )
        total[t, count:count + state, 0:wide] = -part[0:state]

    def tile_of(l):
        return l * rank_top // LANES

    def tile_used(l, t):
        used = bits[0] < 0
        for c in range(l + 1, levels):
            if tile_of(c) == t:
                used = jnp.logical_or(used, bits[c] == 0)
        return used

    def row_block(m):
        if m is None:
            return pl.ds(0, count)
        return pl.ds(count + m * rank_top, rank_top)

    def copies(l):
        out = []
        last = (1 << l) - 1
        first = lax.div(me, 2 << l) * (2 << l) + (1 << l)
        for place in range(last, -1, -1):
            for m in [None] + list(range(l + 1, levels)):
                for t in range(tiles):
                    if t != tile_of(l) and (place != last or all(tile_of(c) != t for c in range(l + 1, levels))):
                        continue
                    condition = []
                    if m is not None:
                        condition.append(bits[m] == 1)
                    if t != tile_of(l):
                        condition.append(tile_used(l, t))
                    slot = 0 if m is None else m + 1
                    out.append((place, condition, pltpu.make_async_remote_copy(
                        src_ref=total.at[t, row_block(m), :],
                        dst_ref=got.at[l, t, row_block(m), :],
                        send_sem=send_sem.at[len(out)],
                        recv_sem=got_sem.at[l, t, slot],
                        device_id={"leaf": first + place},
                        device_id_type=pl.DeviceIdType.MESH,
                    )))
        return out

    def guarded(conditions, action):
        if conditions:
            pl.when(functools.reduce(jnp.logical_and, conditions))(action)
        else:
            action()

    def receive(l):
        for place, condition, copy in copies(l):
            if place != (1 << l) - 1:
                continue
            guarded(condition, copy.wait_recv)

    def receive_narrow(l):
        t = tile_of(l)
        for m in [None] + list(range(l + 1, levels)):
            copy = pltpu.make_async_remote_copy(
                src_ref=total.at[t, row_block(m), :],
                dst_ref=got.at[l, t, row_block(m), :],
                send_sem=send_sem.at[0],
                recv_sem=got_sem.at[l, t, 0 if m is None else m + 1],
                device_id={"leaf": sender_of(l)},
                device_id_type=pl.DeviceIdType.MESH,
            )
            guarded([] if m is None else [bits[m] == 1], copy.wait_recv)

    def level_rows(l, sources):
        own = tile_of(l)
        start = l * rank_top - own * LANES
        row = lax.broadcasted_iota(jnp.int32, (LANES, LANES), 0)
        inside = jnp.logical_and(row >= start, row < start + rank_top)
        at = slice(count + own * LANES, count + (own + 1) * LANES)
        parts = [jnp.where(inside, ref[at, :], 0.0) for ref in sources]
        return split(jnp.concatenate(parts, axis=1))

    def for_rows(l, update):
        update(slice(0, count))
        if l + 1 < levels:
            @pl.when(lax.div(me, 2 << l) > 0)
            def _():
                update(slice(count + (l + 1) * rank_top, count + state))

    def tiles_above(l):
        return sorted({tile_of(c) for c in range(l + 1, levels)})

    def join(l, factors):
        def update(at):
            step = dot_split(got[l, tile_of(l), at, :], factors)
            for place, t in enumerate(tiles_above(l)):
                mine = step[:, place * LANES:(place + 1) * LANES]
                total[t, at, :] = total[t, at, :] + got[l, t, at, :] + mine

        for_rows(l, update)

    def absorb(l, factors):
        def update(at):
            step = dot_split(got[l, tile_of(l), at, :], factors)
            for c in range(l):
                t = tile_of(c)
                got[c, t, at, :] = got[c, t, at, :] + step[:, c * LANES:(c + 1) * LANES]

        for_rows(l, update)

    def below(l):
        return level_rows(l, [got.at[c, tile_of(c)] for c in range(l)])

    for l in range(levels):
        sends = jnp.logical_and(is_last(l), bits[l] == 0)
        if l:
            takes = jnp.logical_and(is_last(l), bits[l] == 1)
            others = jnp.logical_and(jnp.logical_not(is_last(l)), bits[l] == 1)
        else:
            takes, others = bits[l] == 1, None

        @pl.when(sends)
        def _():
            pl.semaphore_wait(barrier, 1 << l)
            for _, condition, copy in copies(l):
                guarded(condition, copy.start)

        if l > 1:
            @pl.when(bits[l - 1] == 1)
            def _():
                absorb(l - 1, below(l - 1))

        if l == levels - 1:
            @pl.when(bits[l] == 1)
            def _():
                factors = below(l) if l else None
                receive_narrow(l)
                if l:
                    absorb(l, factors)

            continue

        @pl.when(takes)
        def _():
            factors = level_rows(l, [total.at[t] for t in tiles_above(l)])
            receive(l)
            join(l, factors)

        if others is not None:
            @pl.when(others)
            def _():
                receive_narrow(l)

    lane = lax.broadcasted_iota(jnp.int32, (1, LANES), 1)
    parts = [jnp.zeros((count, LANES), F32)] * tiles
    for l in range(levels):
        t = tile_of(l)
        start = l * rank_top - t * LANES
        inside = jnp.logical_and(lane >= start, lane < start + rank_top)
        parts[t] = jnp.where(inside, got[l, t, 0:count, :], parts[t])
    p = jnp.concatenate(parts, axis=1)[:, 0:state]
    high = p.astype(BF16).astype(F32)
    both = jnp.concatenate([high, p - high], axis=0).astype(BF16)
    moved = dot(both, wt_ref[...])
    moved_ref[...] = moved[0:count] + moved[count:2 * count]

    for l in range(levels):
        @pl.when(jnp.logical_and(is_last(l), bits[l] == 0))
        def _():
            for _, condition, copy in copies(l):
                guarded(condition, copy.wait_send)


def on_device(rhs_vectors, diag_inverse, left_factors, right_factors, ranks):
    leaves = lax.axis_size("leaf")
    levels = leaves.bit_length() - 1
    count, rows = rhs_vectors.shape
    state = left_factors.shape[1]
    rank_top = state // levels
    tiles = pl.cdiv(state, LANES)
    most = 0
    for l in range(levels):
        most = max(most, ((1 << l) - 1 + tiles) * (levels - l))
    vmem = pl.BlockSpec(memory_space=pltpu.VMEM)
    joined = jnp.concatenate([left_factors.T, rhs_vectors, rhs_vectors], axis=0)
    mapped = lax.dot_general(
        joined, diag_inverse, (((1,), (1,)), ((), ())), preferred_element_type=F32
    )
    base, moved = pl.pallas_call(
        functools.partial(kernel, levels, rank_top),
        out_shape=[jax.ShapeDtypeStruct((count, rows), F32)] * 2,
        in_specs=[pl.BlockSpec(memory_space=pltpu.SMEM), vmem, vmem],
        out_specs=[vmem, vmem],
        scratch_shapes=[
            pltpu.VMEM((state, rows), BF16),
            pltpu.VMEM((tiles, count + tiles * LANES, LANES), F32),
            pltpu.VMEM((levels, tiles, count + tiles * LANES, LANES), F32),
            pltpu.SemaphoreType.DMA((most,)),
            pltpu.SemaphoreType.DMA((levels, tiles, levels + 1)),
        ],
        compiler_params=pltpu.CompilerParams(
            collective_id=0, has_side_effects=True, vmem_limit_bytes=50 * 1024 * 1024
        ),
        cost_estimate=pl.CostEstimate(
            flops=2 * rows * state * (state + 2 * count),
            bytes_accessed=6 * rows * state,
            transcendentals=0,
        ),
    )(ranks, mapped, right_factors.T)
    return base - moved


def solution(mesh):
    in_specs = (P("rhs", "leaf"), P("leaf", None), P("leaf", None), P("leaf", None), P())
    return jax.shard_map(
        on_device, mesh=mesh, in_specs=in_specs, out_specs=P("rhs", "leaf"), check_vma=False
    )
```

```python
import functools

import jax
import jax.numpy as jnp
from jax import lax
from jax.experimental import pallas as pl
from jax.experimental.pallas import tpu as pltpu
from jax.sharding import PartitionSpec as P

LANES = 128
F32 = jnp.float32
BF16 = jnp.bfloat16


def split(x):
    high = x.astype(BF16)
    return high, (x - high.astype(F32)).astype(BF16)


def dot(a, b):
    return jnp.dot(a, b, preferred_element_type=F32)


def dot_turned(a, b):
    return lax.dot_general(a, b, (((1,), (1,)), ((), ())), preferred_element_type=F32)


def dot_split(a, b):
    a_high, a_low = split(a)
    b_high, b_low = split(b)
    return dot(a_high, b_high) + (dot(a_high, b_low) + dot(a_low, b_high))


def kernel(
    levels, rank_top, chunk,
    ranks_ref, b_ref, block_ref, d_hbm, u_hbm, v_hbm, c_ref, moved_ref,
    d_buf, v_buf, x_ref, wt_ref, r_ref, total, got,
    d_sem, u_sem, v_sem, send_sem, got_sem,
):
    me = lax.axis_index("leaf")
    rows = d_buf.shape[0]
    chunks = rows // chunk
    state = v_buf.shape[0]
    count = b_ref.shape[0]
    tiles = total.shape[0]
    bits = [lax.rem(lax.div(me, 1 << l), 2) for l in range(levels)]

    pieces = d_sem.shape[0]
    piece = rows // pieces
    flight = 3
    per = chunk // piece

    def d_copy(m):
        at = pl.ds(m * piece, piece)
        return pltpu.make_async_copy(d_hbm.at[at, :], d_buf.at[at, :], d_sem.at[m])

    u_copy = pltpu.make_async_copy(u_hbm, x_ref.at[pl.ds(0, state), :], u_sem)
    v_copy = pltpu.make_async_copy(v_hbm, v_buf, v_sem)
    u_copy.start()
    for m in range(per, per + flight):
        d_copy(m).start()
    v_copy.start()

    def sender_of(l):
        span = 2 << l
        return lax.div(me, span) * span + ((1 << l) - 1)

    def is_last(l):
        return lax.rem(me, 1 << l) == (1 << l) - 1

    got[...] = jnp.zeros_like(got)
    total[...] = jnp.zeros_like(total)
    barrier = pltpu.get_barrier_semaphore()
    for l in range(levels):
        @pl.when(bits[l] == 1)
        def _():
            pl.semaphore_signal(
                barrier, inc=1, device_id={"leaf": sender_of(l)},
                device_id_type=pl.DeviceIdType.MESH,
            )

    b = b_ref[...].astype(F32)
    x_ref[state:state + 2 * count, :] = jnp.concatenate([b, b], axis=0).astype(BF16)
    u_copy.wait()
    r_ref[...] = jnp.zeros_like(r_ref)

    def multiply(m):
        at = pl.ds(m * chunk, chunk)
        return dot_turned(x_ref[...], d_buf[at, :])

    def project(m, block):
        at = pl.ds(m * chunk, chunk)
        w = block[0:state].astype(BF16)
        twice = block[state:state + 2 * count]
        c_ref[:, at] = twice[0:count]
        high = twice.astype(BF16).astype(F32)
        row = lax.broadcasted_iota(jnp.int32, twice.shape, 0)
        both = jnp.where(row < count, high, twice - high).astype(BF16)
        wt_ref[:, at] = w
        r_ref[...] += dot_turned(jnp.concatenate([w, both], axis=0), v_buf[:, at])

    block = block_ref[...]
    for m in range(1, chunks):
        for part in range(m * per, (m + 1) * per):
            d_copy(part).wait()
            if part + flight < pieces:
                d_copy(part + flight).start()
        if m == 1:
            v_copy.wait()
        after = multiply(m)
        project(m - 1, block)
        block = after
    project(chunks - 1, block)

    lane = lax.broadcasted_iota(jnp.int32, (1, state), 1)
    limit = jnp.zeros((1, state), jnp.int32)
    for l in range(levels):
        limit = jnp.where(lane // rank_top == l, ranks_ref[l], limit)
    r = jnp.where(lane % rank_top < limit, r_ref[...], 0.0)
    for t in range(tiles):
        wide = min(LANES, state - t * LANES)
        part = r[:, t * LANES:t * LANES + wide]
        total[t, 0:count, 0:wide] = (
            part[state:state + count] + part[state + count:state + 2 * count]
        )
        total[t, count:count + state, 0:wide] = -part[0:state]

    def tile_of(l):
        return l * rank_top // LANES

    def tile_used(l, t):
        used = bits[0] < 0
        for c in range(l + 1, levels):
            if tile_of(c) == t:
                used = jnp.logical_or(used, bits[c] == 0)
        return used

    def row_block(m):
        if m is None:
            return pl.ds(0, count)
        return pl.ds(count + m * rank_top, rank_top)

    def copies(l):
        out = []
        last = (1 << l) - 1
        first = lax.div(me, 2 << l) * (2 << l) + (1 << l)
        for place in range(last, -1, -1):
            for m in [None] + list(range(l + 1, levels)):
                for t in range(tiles):
                    if t != tile_of(l) and (place != last or all(tile_of(c) != t for c in range(l + 1, levels))):
                        continue
                    condition = []
                    if m is not None:
                        condition.append(bits[m] == 1)
                    if t != tile_of(l):
                        condition.append(tile_used(l, t))
                    slot = 0 if m is None else m + 1
                    out.append((place, condition, pltpu.make_async_remote_copy(
                        src_ref=total.at[t, row_block(m), :],
                        dst_ref=got.at[l, t, row_block(m), :],
                        send_sem=send_sem.at[len(out)],
                        recv_sem=got_sem.at[l, t, slot],
                        device_id={"leaf": first + place},
                        device_id_type=pl.DeviceIdType.MESH,
                    )))
        return out

    def guarded(conditions, action):
        if conditions:
            pl.when(functools.reduce(jnp.logical_and, conditions))(action)
        else:
            action()

    def receive(l):
        for place, condition, copy in copies(l):
            if place != (1 << l) - 1:
                continue
            guarded(condition, copy.wait_recv)

    def receive_narrow(l):
        t = tile_of(l)
        for m in [None] + list(range(l + 1, levels)):
            copy = pltpu.make_async_remote_copy(
                src_ref=total.at[t, row_block(m), :],
                dst_ref=got.at[l, t, row_block(m), :],
                send_sem=send_sem.at[0],
                recv_sem=got_sem.at[l, t, 0 if m is None else m + 1],
                device_id={"leaf": sender_of(l)},
                device_id_type=pl.DeviceIdType.MESH,
            )
            guarded([] if m is None else [bits[m] == 1], copy.wait_recv)

    def join(l):
        own = tile_of(l)
        start = l * rank_top - own * LANES
        row = lax.broadcasted_iota(jnp.int32, (LANES, LANES), 0)
        inside = jnp.logical_and(row >= start, row < start + rank_top)

        def update(lo, hi):
            factor = got[l, own, lo:hi, :]
            for t in range(tiles):
                if all(tile_of(c) != t for c in range(l + 1, levels)):
                    continue
                at = count + own * LANES
                step = jnp.where(inside, total[t, at:at + LANES, :], 0.0)
                total[t, lo:hi, :] = (
                    total[t, lo:hi, :] + got[l, t, lo:hi, :] + dot_split(factor, step)
                )

        update(0, count)
        if l + 1 < levels:
            @pl.when(lax.div(me, 2 << l) > 0)
            def _():
                update(count + (l + 1) * rank_top, count + state)

    def absorb(l):
        own = tile_of(l)
        start = l * rank_top - own * LANES
        row = lax.broadcasted_iota(jnp.int32, (LANES, LANES), 0)
        inside = jnp.logical_and(row >= start, row < start + rank_top)

        def update(lo, hi):
            factor = got[l, own, lo:hi, :]
            for c in range(l):
                t = tile_of(c)
                at = count + own * LANES
                step = jnp.where(inside, got[c, t, at:at + LANES, :], 0.0)
                got[c, t, lo:hi, :] = got[c, t, lo:hi, :] + dot_split(factor, step)

        update(0, count)
        if l + 1 < levels:
            @pl.when(lax.div(me, 2 << l) > 0)
            def _():
                update(count + (l + 1) * rank_top, count + state)

    for l in range(levels):
        sends = jnp.logical_and(is_last(l), bits[l] == 0)
        if l:
            takes = jnp.logical_and(is_last(l), bits[l] == 1)
            others = jnp.logical_and(jnp.logical_not(is_last(l)), bits[l] == 1)
        else:
            takes, others = bits[l] == 1, None

        @pl.when(sends)
        def _():
            pl.semaphore_wait(barrier, 1 << l)
            for _, condition, copy in copies(l):
                guarded(condition, copy.start)

        if l > 1:
            pl.when(bits[l - 1] == 1)(functools.partial(absorb, l - 1))

        @pl.when(takes)
        def _():
            receive(l)
            if l + 1 < levels:
                join(l)

        if others is not None:
            @pl.when(others)
            def _():
                receive_narrow(l)

    pl.when(bits[levels - 1] == 1)(functools.partial(absorb, levels - 1))

    lane = lax.broadcasted_iota(jnp.int32, (1, LANES), 1)
    parts = [jnp.zeros((count, LANES), F32)] * tiles
    for l in range(levels):
        t = tile_of(l)
        start = l * rank_top - t * LANES
        inside = jnp.logical_and(lane >= start, lane < start + rank_top)
        parts[t] = jnp.where(inside, got[l, t, 0:count, :], parts[t])
    p = jnp.concatenate(parts, axis=1)[:, 0:state]
    high = p.astype(BF16).astype(F32)
    both = jnp.concatenate([high, p - high], axis=0).astype(BF16)
    moved = dot(both, wt_ref[...])
    moved_ref[...] = moved[0:count] + moved[count:2 * count]

    for l in range(levels):
        @pl.when(jnp.logical_and(is_last(l), bits[l] == 0))
        def _():
            for _, condition, copy in copies(l):
                guarded(condition, copy.wait_send)


def on_device(rhs_vectors, diag_inverse, left_factors, right_factors, ranks):
    leaves = lax.axis_size("leaf")
    levels = leaves.bit_length() - 1
    count, rows = rhs_vectors.shape
    state = left_factors.shape[1]
    rank_top = state // levels
    tiles = pl.cdiv(state, LANES)
    chunk = rows // 4
    most = 0
    for l in range(levels):
        most = max(most, ((1 << l) - 1 + tiles) * (levels - l))
    joined = jnp.concatenate([left_factors.T, rhs_vectors, rhs_vectors], axis=0)
    mapped = lax.dot_general(
        joined, diag_inverse[:chunk], (((1,), (1,)), ((), ())), preferred_element_type=F32
    )
    vmem = pl.BlockSpec(memory_space=pltpu.VMEM)
    hbm = pl.BlockSpec(memory_space=pltpu.HBM)
    base, moved = pl.pallas_call(
        functools.partial(kernel, levels, rank_top, chunk),
        out_shape=[jax.ShapeDtypeStruct((count, rows), F32)] * 2,
        in_specs=[pl.BlockSpec(memory_space=pltpu.SMEM), vmem, vmem, hbm, hbm, hbm],
        out_specs=[vmem, vmem],
        scratch_shapes=[
            pltpu.VMEM(diag_inverse.shape, BF16),
            pltpu.VMEM((state, rows), BF16),
            pltpu.VMEM((state + 2 * count, rows), BF16),
            pltpu.VMEM((state, rows), BF16),
            pltpu.VMEM((state + 2 * count, state), F32),
            pltpu.VMEM((tiles, count + tiles * LANES, LANES), F32),
            pltpu.VMEM((levels, tiles, count + tiles * LANES, LANES), F32),
            pltpu.SemaphoreType.DMA((8,)),
            pltpu.SemaphoreType.DMA,
            pltpu.SemaphoreType.DMA,
            pltpu.SemaphoreType.DMA((most,)),
            pltpu.SemaphoreType.DMA((levels, tiles, levels + 1)),
        ],
        compiler_params=pltpu.CompilerParams(
            collective_id=0, has_side_effects=True, vmem_limit_bytes=52 * 1024 * 1024
        ),
        cost_estimate=pl.CostEstimate(
            flops=2 * rows * rows * (state + count), bytes_accessed=2 * rows * (rows + 2 * state), transcendentals=0
        ),
    )(ranks, rhs_vectors, mapped, diag_inverse, left_factors.T, right_factors.T)
    return base - moved


def solution(mesh):
    in_specs = (P("rhs", "leaf"), P("leaf", None), P("leaf", None), P("leaf", None), P())
    return jax.shard_map(
        on_device, mesh=mesh, in_specs=in_specs, out_specs=P("rhs", "leaf"), check_vma=False
    )
```

```python
import functools

import jax
import jax.numpy as jnp
from jax import lax
from jax.experimental import pallas as pl
from jax.experimental.pallas import tpu as pltpu
from jax.sharding import PartitionSpec as P

LANES = 128
F32 = jnp.float32
BF16 = jnp.bfloat16


def split(x):
    high = x.astype(BF16)
    return high, (x - high.astype(F32)).astype(BF16)


def dot(a, b):
    return jnp.dot(a, b, preferred_element_type=F32)


def dot_turned(a, b):
    return lax.dot_general(a, b, (((1,), (1,)), ((), ())), preferred_element_type=F32)


def dot_split(a, b):
    n = a.shape[0]
    high = a.astype(BF16).astype(F32)
    both = jnp.concatenate([high, a - high], axis=0).astype(BF16)
    whole = dot(both, b[0]) + dot(both, b[1])
    return whole[0:n] + whole[n:2 * n]


def kernel(
    levels, rank_top,
    ranks_ref, block_ref, v_ref, moved_ref,
    wt_ref, total, got, send_sem, got_sem,
):
    me = lax.axis_index("leaf")
    state, rows = v_ref.shape
    count = moved_ref.shape[0]
    tiles = total.shape[0]
    bits = [lax.rem(lax.div(me, 1 << l), 2) for l in range(levels)]

    def sender_of(l):
        span = 2 << l
        return lax.div(me, span) * span + ((1 << l) - 1)

    def is_last(l):
        return lax.rem(me, 1 << l) == (1 << l) - 1

    got[...] = jnp.zeros_like(got)
    total[...] = jnp.zeros_like(total)
    barrier = pltpu.get_barrier_semaphore()
    for l in range(levels):
        @pl.when(bits[l] == 1)
        def _():
            pl.semaphore_signal(
                barrier, inc=1, device_id={"leaf": sender_of(l)},
                device_id_type=pl.DeviceIdType.MESH,
            )

    w = block_ref[0:state, :].astype(BF16)
    wt_ref[...] = w
    twice = block_ref[state:state + 2 * count, :]
    high = twice.astype(BF16).astype(F32)
    row = lax.broadcasted_iota(jnp.int32, twice.shape, 0)
    both = jnp.where(row < count, high, twice - high).astype(BF16)
    r = dot_turned(jnp.concatenate([w, both], axis=0), v_ref[...])

    lane = lax.broadcasted_iota(jnp.int32, (1, state), 1)
    limit = jnp.zeros((1, state), jnp.int32)
    for l in range(levels):
        limit = jnp.where(lane // rank_top == l, ranks_ref[l], limit)
    r = jnp.where(lane % rank_top < limit, r, 0.0)
    for t in range(tiles):
        wide = min(LANES, state - t * LANES)
        part = r[:, t * LANES:t * LANES + wide]
        total[t, 0:count, 0:wide] = (
            part[state:state + count] + part[state + count:state + 2 * count]
        )
        total[t, count:count + state, 0:wide] = -part[0:state]

    def tile_of(l):
        return l * rank_top // LANES

    def tile_used(l, t):
        used = bits[0] < 0
        for c in range(l + 1, levels):
            if tile_of(c) == t:
                used = jnp.logical_or(used, bits[c] == 0)
        return used

    def row_block(m):
        if m is None:
            return pl.ds(0, count)
        return pl.ds(count + m * rank_top, rank_top)

    def copies(l):
        out = []
        last = (1 << l) - 1
        first = lax.div(me, 2 << l) * (2 << l) + (1 << l)
        for place in range(last, -1, -1):
            for m in [None] + list(range(l + 1, levels)):
                for t in range(tiles):
                    if t != tile_of(l) and (place != last or all(tile_of(c) != t for c in range(l + 1, levels))):
                        continue
                    condition = []
                    if m is not None:
                        condition.append(bits[m] == 1)
                    if t != tile_of(l):
                        condition.append(tile_used(l, t))
                    slot = 0 if m is None else m + 1
                    out.append((place, condition, pltpu.make_async_remote_copy(
                        src_ref=total.at[t, row_block(m), :],
                        dst_ref=got.at[l, t, row_block(m), :],
                        send_sem=send_sem.at[len(out)],
                        recv_sem=got_sem.at[l, t, slot],
                        device_id={"leaf": first + place},
                        device_id_type=pl.DeviceIdType.MESH,
                    )))
        return out

    def guarded(conditions, action):
        if conditions:
            pl.when(functools.reduce(jnp.logical_and, conditions))(action)
        else:
            action()

    def receive(l):
        for place, condition, copy in copies(l):
            if place != (1 << l) - 1:
                continue
            guarded(condition, copy.wait_recv)

    def receive_narrow(l):
        t = tile_of(l)
        for m in [None] + list(range(l + 1, levels)):
            copy = pltpu.make_async_remote_copy(
                src_ref=total.at[t, row_block(m), :],
                dst_ref=got.at[l, t, row_block(m), :],
                send_sem=send_sem.at[0],
                recv_sem=got_sem.at[l, t, 0 if m is None else m + 1],
                device_id={"leaf": sender_of(l)},
                device_id_type=pl.DeviceIdType.MESH,
            )
            guarded([] if m is None else [bits[m] == 1], copy.wait_recv)

    def level_rows(l, sources):
        own = tile_of(l)
        start = l * rank_top - own * LANES
        row = lax.broadcasted_iota(jnp.int32, (LANES, LANES), 0)
        inside = jnp.logical_and(row >= start, row < start + rank_top)
        at = slice(count + own * LANES, count + (own + 1) * LANES)
        parts = [jnp.where(inside, ref[at, :], 0.0) for ref in sources]
        return split(jnp.concatenate(parts, axis=1))

    def for_rows(l, update):
        update(slice(0, count))
        if l + 1 < levels:
            @pl.when(lax.div(me, 2 << l) > 0)
            def _():
                update(slice(count + (l + 1) * rank_top, count + state))

    def tiles_above(l):
        return sorted({tile_of(c) for c in range(l + 1, levels)})

    def join(l, factors):
        def update(at):
            step = dot_split(got[l, tile_of(l), at, :], factors)
            for place, t in enumerate(tiles_above(l)):
                mine = step[:, place * LANES:(place + 1) * LANES]
                total[t, at, :] = total[t, at, :] + got[l, t, at, :] + mine

        for_rows(l, update)

    def absorb(l, factors):
        def update(at):
            step = dot_split(got[l, tile_of(l), at, :], factors)
            for c in range(l):
                t = tile_of(c)
                got[c, t, at, :] = got[c, t, at, :] + step[:, c * LANES:(c + 1) * LANES]

        for_rows(l, update)

    def below(l):
        return level_rows(l, [got.at[c, tile_of(c)] for c in range(l)])

    for l in range(levels):
        sends = jnp.logical_and(is_last(l), bits[l] == 0)
        if l:
            takes = jnp.logical_and(is_last(l), bits[l] == 1)
            others = jnp.logical_and(jnp.logical_not(is_last(l)), bits[l] == 1)
        else:
            takes, others = bits[l] == 1, None

        @pl.when(sends)
        def _():
            pl.semaphore_wait(barrier, 1 << l)
            for _, condition, copy in copies(l):
                guarded(condition, copy.start)

        if l > 1:
            @pl.when(bits[l - 1] == 1)
            def _():
                absorb(l - 1, below(l - 1))

        if l == levels - 1:
            @pl.when(bits[l] == 1)
            def _():
                factors = below(l) if l else None
                receive_narrow(l)
                if l:
                    absorb(l, factors)

            continue

        @pl.when(takes)
        def _():
            factors = level_rows(l, [total.at[t] for t in tiles_above(l)])
            receive(l)
            join(l, factors)

        if others is not None:
            @pl.when(others)
            def _():
                receive_narrow(l)

    lane = lax.broadcasted_iota(jnp.int32, (1, LANES), 1)
    parts = [jnp.zeros((count, LANES), F32)] * tiles
    for l in range(levels):
        t = tile_of(l)
        start = l * rank_top - t * LANES
        inside = jnp.logical_and(lane >= start, lane < start + rank_top)
        parts[t] = jnp.where(inside, got[l, t, 0:count, :], parts[t])
    p = jnp.concatenate(parts, axis=1)[:, 0:state]
    high = p.astype(BF16).astype(F32)
    both = jnp.concatenate([high, p - high], axis=0).astype(BF16)
    moved = dot(both, wt_ref[...])
    moved_ref[...] = moved[0:count] + moved[count:2 * count]

    for l in range(levels):
        @pl.when(jnp.logical_and(is_last(l), bits[l] == 0))
        def _():
            for _, condition, copy in copies(l):
                guarded(condition, copy.wait_send)


def on_device(rhs_vectors, diag_inverse, left_factors, right_factors, ranks):
    leaves = lax.axis_size("leaf")
    levels = leaves.bit_length() - 1
    count, rows = rhs_vectors.shape
    state = left_factors.shape[1]
    rank_top = state // levels
    tiles = pl.cdiv(state, LANES)
    most = 0
    for l in range(levels):
        most = max(most, ((1 << l) - 1 + tiles) * (levels - l))
    vmem = pl.BlockSpec(memory_space=pltpu.VMEM)
    joined = jnp.concatenate([left_factors.T, rhs_vectors, rhs_vectors], axis=0)
    mapped = lax.dot_general(
        joined, diag_inverse, (((1,), (1,)), ((), ())), preferred_element_type=F32
    )
    moved = pl.pallas_call(
        functools.partial(kernel, levels, rank_top),
        out_shape=jax.ShapeDtypeStruct((count, rows), F32),
        in_specs=[pl.BlockSpec(memory_space=pltpu.SMEM), vmem, vmem],
        out_specs=vmem,
        scratch_shapes=[
            pltpu.VMEM((state, rows), BF16),
            pltpu.VMEM((tiles, count + tiles * LANES, LANES), F32),
            pltpu.VMEM((levels, tiles, count + tiles * LANES, LANES), F32),
            pltpu.SemaphoreType.DMA((most,)),
            pltpu.SemaphoreType.DMA((levels, tiles, levels + 1)),
        ],
        compiler_params=pltpu.CompilerParams(
            collective_id=0, has_side_effects=True, vmem_limit_bytes=50 * 1024 * 1024
        ),
        cost_estimate=pl.CostEstimate(
            flops=2 * rows * state * (state + 2 * count),
            bytes_accessed=6 * rows * state,
            transcendentals=0,
        ),
    )(ranks, mapped, right_factors.T)
    return mapped[state:state + count] - moved


def solution(mesh):
    in_specs = (P("rhs", "leaf"), P("leaf", None), P("leaf", None), P("leaf", None), P())
    return jax.shard_map(
        on_device, mesh=mesh, in_specs=in_specs, out_specs=P("rhs", "leaf"), check_vma=False
    )
```
